128 devices in a mesh: row: 8 (over z_hi, y), col: 16 (over x, z_lo, core).
Axes of the slice: x: 4, y: 4, z: 4 (z_hi: 2, z_lo: 2; z = z_hi * 2 + z_lo), core: 2. Of those that a mesh axis runs over, the one named last changes fastest.
Arguments:
- prompt: bfloat16 [1024, 16384], P(None, ('row', 'col')), may hold values from -0.031982422 to 0.031982422
- base_weight: bfloat16 [16384, 32768], P('row', 'col'), may hold values from -2 to 2
- factor_left: bfloat16 [16384, 64], P(('row', 'col')), may hold values from -0.046875 to 0.046875
- factor_right: bfloat16 [64, 32768], P('row', 'col'), may hold values from -0.75 to 0.75
- magnitude: float32 [32768], P('col'), may hold values from 64 to 512
Outputs:
- serving_weight: bfloat16 [8, 16384, 4096], P('row', None, 'col')
- prefill_out: bfloat16 [8, 1024, 4096], P('row', None, 'col')
The draws below stay inside these ranges and needn't reach their ends.
All inputs are finite; a program needn't handle non-finite values.
Results may differ from the reference program's by a relative error of at most 0.005.
Values may be sent and summed in bfloat16 or wider, within the bound.
No kernel may reach another device: no remote copies, remote signals or barrier semaphores. Data moves between devices by JAX's collectives and lax.ppermute only.
A program may use at most 192 MiB of HBM per device.

```python
import math
import jax
import jax.numpy as jnp
from jax import lax

D = 16384
FF = 32768
R = 64
TOK = 1024
N_ROW = 8
N_COL = 16


def draw_base_weight(key, part):
    key = jax.random.fold_in(key, 11)
    first = jax.random.fold_in(key, 0)
    second = jax.random.fold_in(key, 1)
    fourth = jax.random.fold_in(key, 3)
    place = jnp.arange(D, dtype=jnp.float32) / D
    column_scale = jnp.exp(jax.random.uniform(fourth, (FF,), jnp.float32, 0.0, math.log(10.0)))
    entries = jax.random.normal(first, (D, FF), jnp.float32)
    row_scale = jnp.power(10.0, place) * jnp.exp(jax.random.uniform(second, (D,), jnp.float32, -0.35, 0.35))
    values = entries * row_scale[:, None] * column_scale[None, :] / (4.6 * math.sqrt(D))
    return jnp.clip(values, -2.0, 2.0).astype(jnp.bfloat16)


def level_of(key, shape, cuts, low, top_value):
    level = 1.0
    for axis_at, parts in cuts:
        draws = jax.random.uniform(jax.random.fold_in(jax.random.fold_in(key, 6), axis_at), (parts,), jnp.float32, low / len(cuts), top_value / len(cuts))
        level = level * jnp.repeat(jnp.exp(draws), shape[axis_at] // parts).reshape((-1,) + (1,) * (len(shape) - 1 - axis_at))
    return level


def centred(rng, extent, deviation, most, pieces=(), held_as=jnp.bfloat16):
    drawn = deviation * jax.random.normal(rng, extent, jnp.float32)
    if pieces:
        drawn = drawn * level_of(rng, extent, pieces, -0.22, 0.18)
    return jnp.clip(drawn, -most, most).astype(held_as)


def setup_inputs(seed: int = 0) -> dict:
    keys = jax.random.split(jax.random.key(seed), 6)
    return {
        "prompt": centred(keys[0], (TOK, D), 0.004, 0.031982422, ((1, 128),)),
        "base_weight": draw_base_weight(jax.random.fold_in(keys[5], 71), 0),
        "factor_left": centred(keys[2], (D, R), D ** -0.5, 0.046875, ((0, 128),)),
        "factor_right": centred(keys[3], (R, FF), R ** -0.5, 0.75, ((0, 8), (1, 16))),
        "magnitude": jnp.clip(jnp.exp(math.log(512.0) - 2.0794415 * jax.random.uniform(keys[4], (FF,), jnp.float32) ** level_of(keys[4], (FF,), ((0, 16),), -0.2, 0.2)), 64.0, 512.0),
    }


def reference(prompt, base_weight, factor_left, factor_right, magnitude):
    width = FF // N_COL
    piece = FF // (N_ROW * N_COL)

    def block(index):
        start = (index * width).astype(jnp.int32)
        base = lax.dynamic_slice_in_dim(base_weight, start, width, 1)
        right = lax.dynamic_slice_in_dim(factor_right, start, width, 1)
        scales = lax.dynamic_slice_in_dim(magnitude, start, width, 0)
        combined = base.astype(jnp.float32) + jnp.dot(factor_left, right, preferred_element_type=jnp.float32)
        squares = lax.optimization_barrier(jnp.sum(combined * combined, axis=0))
        merged = (combined * (scales / jnp.sqrt(squares + 1e-06))[None, :]).astype(jnp.bfloat16)
        product = jnp.dot(prompt, merged, preferred_element_type=jnp.float32).astype(jnp.bfloat16)
        return (merged.reshape(D, N_ROW, piece), product.reshape(TOK, N_ROW, piece))
    weights, outputs = lax.map(block, jnp.arange(N_COL, dtype=jnp.int32))
    serving_weight = jnp.transpose(weights, (2, 1, 0, 3)).reshape(N_ROW, D, FF // N_ROW)
    prefill_out = jnp.transpose(outputs, (2, 1, 0, 3)).reshape(N_ROW, TOK, FF // N_ROW)
    return (serving_weight, prefill_out)
```

```python
import functools

import jax
import jax.numpy as jnp
from jax import lax
from jax.experimental import pallas as pl
from jax.experimental.pallas import tpu as pltpu
from jax.sharding import PartitionSpec as P

AXES = ("row", "col")
SHIFTS = (1, -1, 2)
BLOCK = 2048
WIDE = 256
TOK = 1024
N_COL = 16
MIB = 1024 * 1024
F32 = jnp.float32
BF16 = jnp.bfloat16


def move(a, dz=0, dy=0):
    pairs = []
    for r in range(8):
        zh, y = divmod(r, 4)
        to = ((zh + dz) % 2) * 4 + (y + dy) % 4
        pairs += [(r * N_COL + c, to * N_COL + c) for c in range(N_COL)]
    return lax.ppermute(a, AXES, pairs)


def after(x, dep):
    return lax.optimization_barrier((x, dep))[0]


def params(mib, **kw):
    return pltpu.CompilerParams(vmem_limit_bytes=mib * MIB, **kw)


def join_features(p_ref, whole):
    for c in range(N_COL):
        whole[:, c * 128 : (c + 1) * 128] = p_ref[c]


def own_kernel(idx, p_ref, w_ref, o_ref, whole):
    @pl.when(pl.program_id(0) == 0)
    def _():
        join_features(p_ref, whole)

    @pl.loop(0, 4)
    def _(m):
        rows = pl.ds(pl.multiple_of(m * 256, 256), 256)
        o_ref[0, rows, :] = jnp.dot(whole[rows, :], w_ref[...], preferred_element_type=F32)


def own_product(idx, gathered, base):
    return pl.pallas_call(
        own_kernel,
        out_shape=jax.ShapeDtypeStruct((4, TOK, WIDE), F32),
        grid_spec=pltpu.PrefetchScalarGridSpec(
            num_scalar_prefetch=1,
            grid=(4,),
            in_specs=[
                pl.BlockSpec((N_COL, TOK, 128), lambda g, idx: (0, 0, 0)),
                pl.BlockSpec((BLOCK, WIDE), lambda g, idx: (0, idx[g])),
            ],
            out_specs=pl.BlockSpec((1, TOK, WIDE), lambda g, idx: (g, 0, 0)),
            scratch_shapes=[pltpu.VMEM((TOK, BLOCK), BF16)],
        ),
        compiler_params=params(40),
        cost_estimate=pl.CostEstimate(flops=2 * TOK * BLOCK * 4 * WIDE, bytes_accessed=12 * MIB, transcendentals=0),
        name="own_product",
    )(idx, gathered, base)


def low_rank_kernel(p0_ref, p1_ref, l0_ref, l1_ref, o_ref, total):
    @pl.when(pl.program_id(0) == 0)
    def _():
        total[...] = jnp.zeros_like(total)

    acc = total[...]
    for p_ref, l_ref in ((p0_ref, l0_ref), (p1_ref, l1_ref)):
        packed = l_ref[0]
        left = jnp.concatenate([packed[:, :64], packed[:, 64:]], axis=0)
        acc += jnp.dot(p_ref[0], left, preferred_element_type=F32)
    total[...] = acc

    @pl.when(pl.program_id(0) == N_COL - 1)
    def _():
        o_ref[...] = acc.astype(BF16)


def low_rank(own, par, lefts):
    return pl.pallas_call(
        low_rank_kernel,
        out_shape=jax.ShapeDtypeStruct((TOK, 64), BF16),
        grid=(N_COL,),
        in_specs=[
            pl.BlockSpec((1, TOK, 128), lambda c: (c, 0, 0)),
            pl.BlockSpec((1, TOK, 128), lambda c: (c, 0, 0)),
            pl.BlockSpec((1, 64, 128), lambda c: (c, 0, 0)),
            pl.BlockSpec((1, 64, 128), lambda c: (c, 1, 0)),
        ],
        out_specs=pl.BlockSpec((TOK, 64), lambda c: (0, 0)),
        scratch_shapes=[pltpu.VMEM((TOK, 64), F32)],
        compiler_params=params(24),
        cost_estimate=pl.CostEstimate(flops=4 * TOK * BLOCK * 64, bytes_accessed=9 * MIB, transcendentals=0),
        name="low_rank",
    )(own, par, lefts, lefts)


def pair_kernel(n, idx, p_ref, t_ref, r_ref, part_ref, *refs):
    w_refs, o_refs, whole = refs[:n], refs[n : 2 * n], refs[2 * n]

    @pl.when(pl.program_id(0) == 0)
    def _():
        join_features(p_ref, whole)

    for j in range(n):

        @pl.when(pl.program_id(0) == j)
        def _(j=j):
            @pl.loop(0, 4)
            def _(m):
                rows = pl.ds(pl.multiple_of(m * 256, 256), 256)
                acc = jnp.dot(whole[rows, :], w_refs[j][...], preferred_element_type=F32)
                acc += jnp.dot(t_ref[rows, :], r_ref[...], preferred_element_type=F32)
                o_refs[j][rows, :] = (acc + part_ref[0, rows, :]).astype(o_refs[j].dtype)


def pair_product(idx, first, gathered, t, right, part, weights, dtype):
    n = len(weights)
    return pl.pallas_call(
        functools.partial(pair_kernel, n),
        out_shape=[jax.ShapeDtypeStruct((TOK, WIDE), dtype)] * n,
        grid_spec=pltpu.PrefetchScalarGridSpec(
            num_scalar_prefetch=1,
            grid=(n,),
            in_specs=[
                pl.BlockSpec((N_COL, TOK, 128), lambda g, idx: (0, 0, 0)),
                pl.BlockSpec((TOK, 64), lambda g, idx: (0, 0)),
                pl.BlockSpec((64, WIDE), lambda g, idx: (0, idx[first + g])),
                pl.BlockSpec((1, TOK, WIDE), lambda g, idx: (first + g, 0, 0)),
            ]
            + [pl.BlockSpec((BLOCK, WIDE), lambda g, idx: (0, 0))] * n,
            out_specs=[pl.BlockSpec((TOK, WIDE), lambda g, idx: (0, 0))] * n,
            scratch_shapes=[pltpu.VMEM((TOK, BLOCK), BF16)],
        ),
        compiler_params=params(48),
        cost_estimate=pl.CostEstimate(flops=2 * TOK * BLOCK * n * WIDE, bytes_accessed=(5 + 3 * n) * MIB, transcendentals=0),
        name="pair_product",
    )(idx, gathered, t, right, part, *weights)


def merge_kernel(idx, base, *refs):
    blocks, (lefts, rr_ref, mag_ref, out, scale_ref, raw, comb, left, sems, out_sems) = refs[:7], refs[7:]
    first = pltpu.make_async_copy(lefts, left, sems.at[8])
    first.start()
    col = pl.ds(pl.multiple_of(idx[0] * WIDE, WIDE), WIDE)
    pltpu.make_async_copy(base.at[:, col], raw.at[0], sems.at[0]).start()
    for j in range(7):
        pltpu.make_async_copy(blocks[j], raw.at[j + 1], sems.at[j + 1]).start()
    first.wait()

    def part(i, squares):
        j, h = i // 2, i % 2

        @pl.when(h == 0)
        def _():
            pltpu.make_async_copy(blocks[0], raw.at[j], sems.at[j]).wait()

        factor = left[pl.ds(h * 8, 8), pl.ds(pl.multiple_of(j * 64, 64), 64), :].reshape(512, 128)
        update = jnp.dot(factor, rr_ref[...], preferred_element_type=F32)
        for c in range(8):
            for k in range(2):
                rows = pl.ds(pl.multiple_of(h * 1024 + c * 128 + k * 64, 64), 64)
                value = raw[j, rows, :].astype(F32) + update[c * 64 : (c + 1) * 64, k * WIDE : (k + 1) * WIDE]
                comb[j, rows, :] = value
                squares += (value * value).reshape(8, 8, WIDE).sum(axis=0)
        return squares

    squares = lax.fori_loop(0, 16, part, jnp.zeros((8, WIDE), F32))
    scale = mag_ref[...] / jnp.sqrt(squares.sum(axis=0, keepdims=True) + 1e-6)
    scale_ref[...] = scale

    def out_copy(j):
        rows = pl.ds(pl.multiple_of(idx[4 + j] * BLOCK, BLOCK), BLOCK)
        return pltpu.make_async_copy(raw.at[j], out.at[rows, :], out_sems.at[j])

    @pl.loop(0, 8)
    def _(j):
        @pl.loop(0, 8)
        def _(m):
            rows = pl.ds(pl.multiple_of(m * 256, 256), 256)
            raw[j, rows, :] = (comb[j, rows, :] * scale).astype(BF16)

        out_copy(j).start()

    @pl.loop(0, 8)
    def _(j):
        out_copy(j).wait()


def merge(idx, base, blocks, lefts, rr, mag):
    any_space = pl.BlockSpec(memory_space=pl.ANY)
    vmem = pl.BlockSpec(memory_space=pltpu.VMEM)
    return pl.pallas_call(
        merge_kernel,
        out_shape=[jax.ShapeDtypeStruct((8 * BLOCK, WIDE), BF16), jax.ShapeDtypeStruct((1, WIDE), F32)],
        in_specs=[pl.BlockSpec(memory_space=pltpu.SMEM)] + [any_space] * 9 + [vmem] * 2,
        out_specs=[any_space, vmem],
        scratch_shapes=[
            pltpu.VMEM((8, BLOCK, WIDE), BF16),
            pltpu.VMEM((8, BLOCK, WIDE), F32),
            pltpu.VMEM((N_COL, 512, 128), BF16),
            pltpu.SemaphoreType.DMA((9,)),
            pltpu.SemaphoreType.DMA((8,)),
        ],
        compiler_params=params(48),
        cost_estimate=pl.CostEstimate(flops=2 * 128 * 512 * 8192, bytes_accessed=18 * MIB, transcendentals=0),
        name="merge",
    )(idx, base, *blocks, lefts, rr, mag)


def shards(prompt, base, factor_left, factor_right, magnitude):
    row = lax.axis_index("row").astype(jnp.int32)
    zh, y = row // 4, row % 4

    def served_by(dz, dy):
        return ((zh + dz) % 2) * 4 + (y + dy) % 4

    def cols(dz, dy):
        return lax.dynamic_slice(base, (0, served_by(dz, dy) * WIDE), (BLOCK, WIDE))

    prompt_own = lax.all_gather(prompt, "col", axis=0, tiled=False)

    left = jnp.concatenate([factor_left[:64], factor_left[64:]], axis=1)
    right = factor_right.reshape(8, 16, 128).transpose(1, 0, 2).reshape(128, 128)
    factors = jnp.concatenate([left, right], axis=0)
    from_partner = move(jnp.concatenate([prompt, factors], axis=0), dz=1)
    prompt_par = lax.all_gather(from_partner[:TOK], "col", axis=0, tiled=False)

    straight = {}
    for d in SHIFTS:
        straight[d] = move(cols(0, d), dy=d)

    both = jnp.concatenate([factors, from_partner[TOK:]], axis=0)
    got = {}
    previous = None
    for d in SHIFTS:
        got[d] = move(both if previous is None else after(both, previous), dy=d)
        previous = got[d]
    order = (0,) + SHIFTS
    got[0] = both
    lefts = jnp.concatenate([got[d][k * 192 : k * 192 + 64] for d in order for k in range(2)], axis=0)
    lefts = lax.all_gather(lefts, "col", axis=0, tiled=False)

    rights = jnp.stack([got[d].reshape(2, 192, 128)[:, 64:] for d in (0, -1, 2, 1)])
    rights = lax.dynamic_slice_in_dim(jnp.concatenate([rights, rights], axis=0), (4 - y) % 4, 4, 0)
    rights = lax.dynamic_slice_in_dim(jnp.concatenate([rights, rights[:, :1]], axis=1), zh, 2, 1)
    rights = rights.reshape(4, 2, 16, 8, 128).transpose(1, 0, 3, 2, 4).reshape(64, 2048)

    half = {}
    chain = [from_partner]
    for d in SHIFTS + (0,):
        dep = chain[-1] if len(chain) < 2 else (previous if len(chain) == 2 else chain[-2])
        half[d] = move(after(cols(1, d), dep), dz=1)
        chain.append(half[d])
    relayed = {}
    for d in SHIFTS:
        relayed[d] = move(after(half[d], straight[d]), dy=d)

    idx = jnp.stack([served_by(0, d) for d in order])
    part = own_product(idx, prompt_own, base)
    t = low_rank(prompt_own, prompt_par, lefts)
    sends = pair_product(idx, 1, prompt_par, t, rights, part, [half[d] for d in SHIFTS], BF16)
    (mine,) = pair_product(idx, 0, prompt_par, t, rights, part, [half[0]], F32)
    sums = [move(after(s, relayed[d]), dy=d) for s, d in zip(sends, SHIFTS)]

    places = jnp.stack([((zh + k) % 2) * 4 + (y - d) % 4 for d in order for k in range(2)])
    right_mine = lax.dynamic_slice(rights, (0, row * WIDE), (64, WIDE))
    rr = jnp.pad(right_mine, ((0, 64), (0, WIDE))) + jnp.pad(right_mine, ((64, 0), (WIDE, 0)))
    mag = lax.dynamic_slice(magnitude, (row * WIDE,), (WIDE,))[None]
    blocks = [half[0]]
    for d in SHIFTS:
        blocks += [straight[d], relayed[d]]
    serving, scale = merge(jnp.concatenate([idx, places]), base, blocks, lefts, rr, mag)

    product = mine
    for s in sums:
        product = product + s.astype(F32)
    return serving[None], (product * scale).astype(BF16)[None]


def solution(mesh):
    in_specs = (
        P(None, ("row", "col")),
        P("row", "col"),
        P(("row", "col"), None),
        P("row", "col"),
        P("col"),
    )
    out_specs = (P("row", None, "col"), P("row", None, "col"))
    return jax.shard_map(shards, mesh=mesh, in_specs=in_specs, out_specs=out_specs, check_vma=False)
```

```python
import functools

import jax
import jax.numpy as jnp
from jax import lax
from jax.experimental import pallas as pl
from jax.experimental.pallas import tpu as pltpu
from jax.sharding import PartitionSpec as P

AXES = ("row", "col")
SHIFTS = (1, -1, 2)
BLOCK = 2048
WIDE = 256
TOK = 1024
N_COL = 16
MIB = 1024 * 1024
F32 = jnp.float32
BF16 = jnp.bfloat16


def move(a, dz=0, dy=0):
    pairs = []
    for r in range(8):
        zh, y = divmod(r, 4)
        to = ((zh + dz) % 2) * 4 + (y + dy) % 4
        pairs += [(r * N_COL + c, to * N_COL + c) for c in range(N_COL)]
    return lax.ppermute(a, AXES, pairs)


def swap(a, bits):
    return lax.ppermute(a, AXES, [(i, i ^ bits) for i in range(128)])


def gather_x(a):
    groups = [[16 * r + 4 * x + k for x in range(4)] for r in range(8) for k in range(4)]
    return lax.all_gather(a, AXES, axis=0, tiled=False, axis_index_groups=groups)


def after(x, *deps):
    return lax.optimization_barrier((x, *deps))[0]


def params(mib, **kw):
    return pltpu.CompilerParams(vmem_limit_bytes=mib * MIB, **kw)


PART = TOK + 64
PLACE = dict(served=0, rows=4, zl=12, core=13)


def block_copies(idx, mine, other, whole, left, sem, left_sem):
    prompts, lefts = [], []
    for x in range(4):
        for h in range(2):
            for src, k in ((mine, idx[PLACE["core"]]), (other, 1 - idx[PLACE["core"]])):
                zl = idx[PLACE["zl"]] if h == 0 else 1 - idx[PLACE["zl"]]
                c = x * 4 + zl * 2 + k
                lanes = pl.ds(pl.multiple_of(c * 128, 128), 128)
                prompts.append(pltpu.make_async_copy(src.at[x, pl.ds(h * PART, TOK), :], whole.at[:, lanes], sem))
                if left is not None:
                    lefts.append(pltpu.make_async_copy(src.at[x, pl.ds(h * PART + TOK, 64), :], left.at[c], left_sem))
    return prompts, lefts


EXTRA = 96


def pack_kernel(n, idx, base, *refs):
    factors, outs, (stage, sems) = refs[:-n - 2], refs[-n - 2 : -2], refs[-2:]
    reads, writes = [], []
    for j in range(n):
        at = pl.ds(pl.multiple_of(idx[j] * WIDE, WIDE), WIDE)
        for h in range(2):
            rows = pl.ds(h * 1024, 1024)
            reads.append([pltpu.make_async_copy(base.at[rows, at], stage.at[j, rows, :], sems.at[0, j, h])])
            writes.append(pltpu.make_async_copy(stage.at[j, rows, :], outs[j].at[rows, :], sems.at[1, j, h]))
        if factors:
            rows = pl.ds(BLOCK, EXTRA)
            reads.append(
                [
                    pltpu.make_async_copy(
                        factors[0].at[pl.ds(h * EXTRA, EXTRA), :], stage.at[j, rows, pl.ds(h * 128, 128)], sems.at[0, j, 2]
                    )
                    for h in range(2)
                ]
            )
            writes.append(pltpu.make_async_copy(stage.at[j, rows, :], outs[j].at[rows, :], sems.at[1, j, 2]))
    for group in reads:
        for c in group:
            c.start()
    for group, w in zip(reads, writes):
        wait_all(group)
        w.start()
    wait_all(writes)


def pack(places, base, *factors):
    n, rows = len(places), BLOCK + (EXTRA if factors else 0)
    return pl.pallas_call(
        functools.partial(pack_kernel, n),
        out_shape=[jax.ShapeDtypeStruct((rows, WIDE), BF16)] * n,
        in_specs=specs("sh" + "h" * len(factors)),
        out_specs=specs("h" * n),
        scratch_shapes=[pltpu.VMEM((n, rows, WIDE), BF16), pltpu.SemaphoreType.DMA((2, n, 3))],
        compiler_params=params(56),
        cost_estimate=pl.CostEstimate(flops=0, bytes_accessed=2 * n * MIB, transcendentals=0),
        name="pack",
    )(jnp.stack(places), base, *factors)


def wait_all(copies):
    for c in copies:
        c.wait()


def specs(kinds):
    space = dict(h=pltpu.HBM, s=pltpu.SMEM, v=pltpu.VMEM)
    return [pl.BlockSpec(memory_space=space[k]) for k in kinds]


def dot(a, b):
    return jnp.dot(a, b, preferred_element_type=F32)


def unpacked(ref):
    value = ref[...]
    return jnp.concatenate([value[:, :, :64], value[:, :, 64:]], axis=1).reshape(BLOCK, 64)


def own_kernel(idx, mine, other, base, acc, t_ref, own, w, left, sems):
    prompts, lefts = block_copies(idx, mine, other, own, left, sems.at[4], sems.at[5])
    cols = []
    for j in range(4):
        at = pl.ds(pl.multiple_of(idx[j] * WIDE, WIDE), WIDE)
        cols.append(pltpu.make_async_copy(base.at[:, at], w.at[j], sems.at[j]))
    for c in lefts + prompts + cols:
        c.start()
    wait_all(lefts)
    factor = unpacked(left)
    wait_all(prompts)
    t_ref[...] = dot(own[...], factor)
    for j in range(4):
        cols[j].wait()
        acc[j] = dot(own[...], w[j])


def own_part(idx, mine, other, base):
    return pl.pallas_call(
        own_kernel,
        out_shape=[jax.ShapeDtypeStruct((4, TOK, WIDE), F32), jax.ShapeDtypeStruct((TOK, 64), F32)],
        in_specs=specs("shhh"),
        out_specs=specs("vv"),
        scratch_shapes=[
            pltpu.VMEM((TOK, BLOCK), BF16),
            pltpu.VMEM((4, BLOCK, WIDE), BF16),
            pltpu.VMEM((N_COL, 64, 128), BF16),
            pltpu.SemaphoreType.DMA((6,)),
        ],
        compiler_params=params(56),
        cost_estimate=pl.CostEstimate(flops=2 * TOK * BLOCK * 5 * WIDE, bytes_accessed=13 * MIB, transcendentals=0),
        name="own_part",
    )(idx, mine, other, base)


def partner_kernel(idx, mine, other, h1, h2, h3, r_ref, own_t, acc, o1, o2, o3, t_ref, par, w, part, left, sems):
    prompts, lefts = block_copies(idx, mine, other, par, left, sems.at[6], sems.at[7])
    halves = [pltpu.make_async_copy(h, w.at[i], sems.at[i]) for i, h in enumerate((h1, h2, h3))]
    parts = [pltpu.make_async_copy(acc.at[i + 1], part.at[i], sems.at[3 + i]) for i in range(3)]
    for c in lefts + prompts:
        c.start()
    for h, p in zip(halves, parts):
        h.start()
        p.start()
    wait_all(lefts)
    factor = unpacked(left)
    wait_all(prompts)
    t = (own_t[...] + dot(par[...], factor)).astype(BF16)
    t_ref[...] = t
    for i, o in enumerate((o1, o2, o3)):
        right = r_ref[:, pl.ds(pl.multiple_of(idx[1 + i] * WIDE, WIDE), WIDE)]
        halves[i].wait()
        parts[i].wait()
        o[...] = (dot(par[...], w[i]) + dot(t, right) + part[i]).astype(BF16)


def partner_part(idx, mine, other, halves, rights, own_t, acc):
    send = jax.ShapeDtypeStruct((TOK, WIDE), BF16)
    return pl.pallas_call(
        partner_kernel,
        out_shape=[send, send, send, jax.ShapeDtypeStruct((TOK, 64), BF16)],
        in_specs=specs("shhhhhvvh"),
        out_specs=specs("vvvv"),
        scratch_shapes=[
            pltpu.VMEM((TOK, BLOCK), BF16),
            pltpu.VMEM((3, BLOCK, WIDE), BF16),
            pltpu.VMEM((3, TOK, WIDE), F32),
            pltpu.VMEM((N_COL, 64, 128), BF16),
            pltpu.SemaphoreType.DMA((8,)),
        ],
        compiler_params=params(56),
        cost_estimate=pl.CostEstimate(flops=2 * TOK * BLOCK * 4 * WIDE, bytes_accessed=12 * MIB, transcendentals=0),
        name="partner_part",
    )(idx, mine, other, *halves, rights, own_t, acc)


def last_kernel(idx, mine, other, half, t_ref, r_ref, acc, o, par, w, part, sems):
    copies, _ = block_copies(idx, mine, other, par, None, sems.at[0], None)
    copies.append(pltpu.make_async_copy(half, w, sems.at[1]))
    copies.append(pltpu.make_async_copy(acc.at[0], part, sems.at[2]))
    for c in copies:
        c.start()
    wait_all(copies)
    right = r_ref[:, pl.ds(pl.multiple_of(idx[0] * WIDE, WIDE), WIDE)]
    o[...] = dot(par[...], w[...]) + dot(t_ref[...], right) + part[...]


def last_part(idx, mine, other, half, t, rights, acc):
    return pl.pallas_call(
        last_kernel,
        out_shape=jax.ShapeDtypeStruct((TOK, WIDE), F32),
        in_specs=specs("shhhvvh"),
        out_specs=specs("v")[0],
        scratch_shapes=[
            pltpu.VMEM((TOK, BLOCK), BF16),
            pltpu.VMEM((BLOCK, WIDE), BF16),
            pltpu.VMEM((TOK, WIDE), F32),
            pltpu.SemaphoreType.DMA((3,)),
        ],
        compiler_params=params(56),
        cost_estimate=pl.CostEstimate(flops=2 * TOK * BLOCK * WIDE, bytes_accessed=7 * MIB, transcendentals=0),
        name="last_part",
    )(idx, mine, other, half, t, rights, acc)


def merge_kernel(idx, base, *refs):
    blocks, (lefts, rr_ref, mag_ref, out, scale_ref, raw, comb, left, sems, out_sems) = refs[:7], refs[7:]
    first = [pltpu.make_async_copy(lefts, left, sems.at[8])]
    for c in first:
        c.start()
    col = pl.ds(pl.multiple_of(idx[0] * WIDE, WIDE), WIDE)
    pltpu.make_async_copy(base.at[:, col], raw.at[0], sems.at[0]).start()
    for j in range(7):
        pltpu.make_async_copy(blocks[j].at[pl.ds(0, BLOCK), :], raw.at[j + 1], sems.at[j + 1]).start()
    wait_all(first)

    def part(i, squares):
        j, h = i // 2, i % 2

        @pl.when(h == 0)
        def _():
            pltpu.make_async_copy(blocks[0], raw.at[j], sems.at[j]).wait()

        factor = left[pl.ds(h * 8, 8), pl.ds(pl.multiple_of(j * 64, 64), 64), :].reshape(512, 128)
        update = jnp.dot(factor, rr_ref[...], preferred_element_type=F32)
        for c in range(8):
            for k in range(2):
                rows = pl.ds(pl.multiple_of(h * 1024 + c * 128 + k * 64, 64), 64)
                value = raw[j, rows, :].astype(F32) + update[c * 64 : (c + 1) * 64, k * WIDE : (k + 1) * WIDE]
                comb[j, rows, :] = value
                squares += (value * value).reshape(8, 8, WIDE).sum(axis=0)
        return squares

    squares = lax.fori_loop(0, 16, part, jnp.zeros((8, WIDE), F32))
    scale = mag_ref[...] / jnp.sqrt(squares.sum(axis=0, keepdims=True) + 1e-6)
    scale_ref[...] = scale

    def out_copy(j):
        rows = pl.ds(pl.multiple_of(idx[PLACE["rows"] + j] * BLOCK, BLOCK), BLOCK)
        return pltpu.make_async_copy(raw.at[j], out.at[rows, :], out_sems.at[j])

    @pl.loop(0, 8)
    def _(j):
        @pl.loop(0, 8)
        def _(m):
            rows = pl.ds(pl.multiple_of(m * 256, 256), 256)
            raw[j, rows, :] = (comb[j, rows, :] * scale).astype(BF16)

        out_copy(j).start()

    @pl.loop(0, 8)
    def _(j):
        out_copy(j).wait()


def merge(idx, base, blocks, lefts, rr, mag):
    any_space = pl.BlockSpec(memory_space=pltpu.HBM)
    vmem = pl.BlockSpec(memory_space=pltpu.VMEM)
    return pl.pallas_call(
        merge_kernel,
        out_shape=[jax.ShapeDtypeStruct((8 * BLOCK, WIDE), BF16), jax.ShapeDtypeStruct((1, WIDE), F32)],
        in_specs=[pl.BlockSpec(memory_space=pltpu.SMEM)] + [any_space] * 9 + [vmem] * 2,
        out_specs=[any_space, vmem],
        scratch_shapes=[
            pltpu.VMEM((8, BLOCK, WIDE), BF16),
            pltpu.VMEM((8, BLOCK, WIDE), F32),
            pltpu.VMEM((N_COL, 512, 128), BF16),
            pltpu.SemaphoreType.DMA((9,)),
            pltpu.SemaphoreType.DMA((8,)),
        ],
        compiler_params=params(56),
        cost_estimate=pl.CostEstimate(flops=2 * 128 * 512 * 8192, bytes_accessed=18 * MIB, transcendentals=0),
        name="merge",
    )(idx, base, *blocks, lefts, rr, mag)


def shards(prompt, base, factor_left, factor_right, magnitude):
    row = lax.axis_index("row").astype(jnp.int32)
    zh, y = row // 4, row % 4
    order = (0,) + SHIFTS

    def served_by(dz, dy):
        return ((zh + dz) % 2) * 4 + (y + dy) % 4

    left = jnp.concatenate([factor_left[:64], factor_left[64:]], axis=1)
    right = factor_right.reshape(8, 16, 128).transpose(1, 0, 2).reshape(128, 128)
    factors = jnp.concatenate([left, right], axis=0)
    small = jnp.concatenate([prompt, left], axis=0)

    partner, beside, beside_partner = swap(small, 64), swap(small, 2), swap(small, 66)
    half, straight, relayed = {}, {}, {}
    packed = dict(zip(SHIFTS, pack([served_by(0, d) for d in SHIFTS], base, factors)))
    packed_half = dict(zip(SHIFTS + (0,), pack([served_by(1, d) for d in SHIFTS + (0,)], base)))

    wave = (partner, beside, beside_partner, packed[2], packed_half[2])
    beside, partner, *_ = wave_end = lax.optimization_barrier((beside, partner, beside_partner, packed[2], packed_half[2]))
    mine = gather_x(jnp.concatenate([small, beside], axis=0))
    mine_partner = gather_x(jnp.concatenate([partner, wave_end[2]], axis=0))
    for d in SHIFTS:
        straight[d] = move(after(packed[d], *wave), dy=d)
    for d in (1, -1):
        half[d] = move(after(packed_half[d], *wave), dz=1)

    wave = (half[1], half[-1], *(straight[d] for d in SHIFTS))
    for d in (1, -1):
        relayed[d] = move(after(half[d], *wave), dy=d)
    half[2] = move(after(packed_half[2], *wave), dz=1)
    got = [factors]
    for d in SHIFTS:
        below = straight[d][BLOCK:]
        got.append(jnp.concatenate([below[:, :128], below[:, 128:]], axis=0))
    got = jnp.stack(got)
    got = jnp.stack([got, move(after(got, *wave), dz=1)], axis=1)
    places = [((zh + k) % 2) * 4 + (y - d) % 4 for d in order for k in range(2)]
    at_col = lax.axis_index("col").astype(jnp.int32)
    idx = jnp.stack([served_by(0, d) for d in order] + places + [at_col // 2 % 2, at_col % 2])
    other = swap(after(mine, *wave), 1)
    acc, own_t = own_part(idx, mine, other, base)

    wave = (half[2], relayed[1], relayed[-1], got, own_t)
    relayed[2] = move(after(half[2], *wave), dy=2)
    half[0] = move(after(packed_half[0], *wave), dz=1)
    other_partner = swap(after(mine_partner, *wave), 1)
    lefts = lax.all_gather(got[:, :, :64].reshape(512, 128), "col", axis=0, tiled=False)

    rights = jnp.stack([got[j, :, 64:] for j in (0, 2, 3, 1)])
    rights = lax.dynamic_slice_in_dim(jnp.concatenate([rights, rights], axis=0), (4 - y) % 4, 4, 0)
    rights = lax.dynamic_slice_in_dim(jnp.concatenate([rights, rights[:, :1]], axis=1), zh, 2, 1)
    rights = rights.reshape(4, 2, 16, 8, 128).transpose(1, 0, 3, 2, 4).reshape(64, 2048)

    *sends, t = partner_part(idx, mine_partner, other_partner, [half[d] for d in SHIFTS], rights, own_t, acc)
    sums = [move(s, dy=d) for s, d in zip(sends, SHIFTS)]

    right_mine = lax.dynamic_slice(rights, (0, row * WIDE), (64, WIDE))
    rr = jnp.pad(right_mine, ((0, 64), (0, WIDE))) + jnp.pad(right_mine, ((64, 0), (WIDE, 0)))
    mag = lax.dynamic_slice(magnitude, (row * WIDE,), (WIDE,))[None]
    blocks = [half[0]]
    for d in SHIFTS:
        blocks += [straight[d], relayed[d]]
    serving, scale = merge(idx, base, blocks, lefts, rr, mag)

    product = last_part(idx, mine_partner, other_partner, half[0], t, rights, acc)
    for s in sums:
        product = product + s.astype(F32)
    return serving[None], (product * scale).astype(BF16)[None]


def solution(mesh):
    in_specs = (
        P(None, ("row", "col")),
        P("row", "col"),
        P(("row", "col"), None),
        P("row", "col"),
        P("col"),
    )
    out_specs = (P("row", None, "col"), P("row", None, "col"))
    return jax.shard_map(shards, mesh=mesh, in_specs=in_specs, out_specs=out_specs, check_vma=False)
```

```python
import functools

import jax
import jax.numpy as jnp
from jax import lax
from jax.experimental import pallas as pl
from jax.experimental.pallas import tpu as pltpu
from jax.sharding import PartitionSpec as P

AXES = ("row", "col")
SHIFTS = (1, -1, 2)
BLOCK = 2048
WIDE = 256
TOK = 1024
N_COL = 16
MIB = 1024 * 1024
F32 = jnp.float32
BF16 = jnp.bfloat16


def move(a, dz=0, dy=0):
    pairs = []
    for r in range(8):
        zh, y = divmod(r, 4)
        to = ((zh + dz) % 2) * 4 + (y + dy) % 4
        pairs += [(r * N_COL + c, to * N_COL + c) for c in range(N_COL)]
    return lax.ppermute(a, AXES, pairs)


def swap(a, bits):
    return lax.ppermute(a, AXES, [(i, i ^ bits) for i in range(128)])


def gather_x(a):
    groups = [[16 * r + 4 * x + 2 * zl + k for x in range(4) for k in range(2)] for r in range(8) for zl in range(2)]
    return lax.all_gather(a, AXES, axis=0, tiled=False, axis_index_groups=groups)


def after(x, *deps):
    return lax.optimization_barrier((x, *deps))[0]


def params(mib, **kw):
    return pltpu.CompilerParams(vmem_limit_bytes=mib * MIB, **kw)


PART = TOK + 64
PLACE = dict(served=0, rows=4, zl=12)


def block_copies(idx, gathered, whole, left, sem, left_sem):
    prompts, lefts = [], []
    for j in range(8):
        for h in range(2):
            zl = idx[PLACE["zl"]] if h == 0 else 1 - idx[PLACE["zl"]]
            c = j // 2 * 4 + zl * 2 + j % 2
            lanes = pl.ds(pl.multiple_of(c * 128, 128), 128)
            prompts.append(pltpu.make_async_copy(gathered.at[j, pl.ds(h * PART, TOK), :], whole.at[:, lanes], sem))
            if left is not None:
                lefts.append(pltpu.make_async_copy(gathered.at[j, pl.ds(h * PART + TOK, 64), :], left.at[c], left_sem))
    return prompts, lefts


EXTRA = 128


def pack_kernel(n, idx, base, *refs):
    outs, (stage, sems) = refs[:-2], refs[-2:]
    reads, writes = [], []
    for j in range(n):
        at = pl.ds(pl.multiple_of(idx[j] * WIDE, WIDE), WIDE)
        for h in range(2):
            rows = pl.ds(h * 1024, 1024)
            reads.append(pltpu.make_async_copy(base.at[rows, at], stage.at[j, rows, :], sems.at[0, j, h]))
            writes.append(pltpu.make_async_copy(stage.at[j, rows, :], outs[j].at[rows, :], sems.at[1, j, h]))
    for c in reads:
        c.start()
    for r, w in zip(reads, writes):
        r.wait()
        w.start()
    wait_all(writes)


def pack(places, base, extra):
    n = len(places)
    return pl.pallas_call(
        functools.partial(pack_kernel, n),
        out_shape=[jax.ShapeDtypeStruct((BLOCK + EXTRA * (j < extra), WIDE), BF16) for j in range(n)],
        in_specs=specs("sh"),
        out_specs=specs("h" * n),
        scratch_shapes=[pltpu.VMEM((n, BLOCK, WIDE), BF16), pltpu.SemaphoreType.DMA((2, n, 2))],
        compiler_params=params(56),
        cost_estimate=pl.CostEstimate(flops=0, bytes_accessed=2 * n * MIB, transcendentals=0),
        name="pack",
    )(jnp.stack(places), base)


def append_kernel(left, beside, right, a1, a2, a3, o1, o2, o3, sem):
    copies = []
    for o in (o1, o2, o3):
        for src, row, lane in ((left, 0, 0), (beside.at[pl.ds(TOK, 64), :], 64, 0), (right, 0, 128)):
            dst = o.at[pl.ds(BLOCK + row, src.shape[0]), pl.ds(lane, 128)]
            copies.append(pltpu.make_async_copy(src, dst, sem))
    for c in copies:
        c.start()
    wait_all(copies)


def append(left, beside, right, blocks):
    return pl.pallas_call(
        append_kernel,
        out_shape=[jax.ShapeDtypeStruct(b.shape, b.dtype) for b in blocks],
        in_specs=specs("vvvhhh"),
        out_specs=specs("hhh"),
        scratch_shapes=[pltpu.SemaphoreType.DMA],
        input_output_aliases={3: 0, 4: 1, 5: 2},
        compiler_params=params(56),
        cost_estimate=pl.CostEstimate(flops=0, bytes_accessed=MIB, transcendentals=0),
        name="append",
    )(left, beside, right, *blocks)


def wait_all(copies):
    for c in copies:
        c.wait()


def specs(kinds):
    space = dict(h=pltpu.HBM, s=pltpu.SMEM, v=pltpu.VMEM)
    return [pl.BlockSpec(memory_space=space[k]) for k in kinds]


def dot(a, b):
    return jnp.dot(a, b, preferred_element_type=F32)


def unpacked(ref):
    value = ref[...]
    return jnp.concatenate([value[:, :, :64], value[:, :, 64:]], axis=1).reshape(BLOCK, 64)


def own_kernel(idx, gathered, base, acc, t_ref, own, w, left, sems):
    prompts, lefts = block_copies(idx, gathered, own, left, sems.at[4], sems.at[5])
    cols = []
    for j in range(4):
        at = pl.ds(pl.multiple_of(idx[j] * WIDE, WIDE), WIDE)
        cols.append(pltpu.make_async_copy(base.at[:, at], w.at[j], sems.at[j]))
    for c in lefts + prompts + cols:
        c.start()
    wait_all(lefts)
    factor = unpacked(left)
    wait_all(prompts)
    t_ref[...] = dot(own[...], factor)
    for j in range(4):
        cols[j].wait()
        acc[j] = dot(own[...], w[j])


def own_part(idx, gathered, base):
    return pl.pallas_call(
        own_kernel,
        out_shape=[jax.ShapeDtypeStruct((4, TOK, WIDE), F32), jax.ShapeDtypeStruct((TOK, 64), F32)],
        in_specs=specs("shh"),
        out_specs=specs("vv"),
        scratch_shapes=[
            pltpu.VMEM((TOK, BLOCK), BF16),
            pltpu.VMEM((4, BLOCK, WIDE), BF16),
            pltpu.VMEM((N_COL, 64, 128), BF16),
            pltpu.SemaphoreType.DMA((6,)),
        ],
        compiler_params=params(56),
        cost_estimate=pl.CostEstimate(flops=2 * TOK * BLOCK * 5 * WIDE, bytes_accessed=13 * MIB, transcendentals=0),
        name="own_part",
    )(idx, gathered, base)


def partner_kernel(idx, gathered, h1, h2, h3, r_ref, own_t, acc, o1, o2, o3, t_ref, par, w, part, left, sems):
    prompts, lefts = block_copies(idx, gathered, par, left, sems.at[6], sems.at[7])
    halves = [pltpu.make_async_copy(h, w.at[i], sems.at[i]) for i, h in enumerate((h1, h2, h3))]
    parts = [pltpu.make_async_copy(acc.at[i + 1], part.at[i], sems.at[3 + i]) for i in range(3)]
    for c in lefts + prompts:
        c.start()
    for h, p in zip(halves, parts):
        h.start()
        p.start()
    wait_all(lefts)
    factor = unpacked(left)
    wait_all(prompts)
    t = (own_t[...] + dot(par[...], factor)).astype(BF16)
    t_ref[...] = t
    for i, o in enumerate((o1, o2, o3)):
        right = r_ref[:, pl.ds(pl.multiple_of(idx[1 + i] * WIDE, WIDE), WIDE)]
        halves[i].wait()
        parts[i].wait()
        o[...] = (dot(par[...], w[i]) + dot(t, right) + part[i]).astype(BF16)


def partner_part(idx, gathered, halves, rights, own_t, acc):
    send = jax.ShapeDtypeStruct((TOK, WIDE), BF16)
    return pl.pallas_call(
        partner_kernel,
        out_shape=[send, send, send, jax.ShapeDtypeStruct((TOK, 64), BF16)],
        in_specs=specs("shhhhvvh"),
        out_specs=specs("vvvv"),
        scratch_shapes=[
            pltpu.VMEM((TOK, BLOCK), BF16),
            pltpu.VMEM((3, BLOCK, WIDE), BF16),
            pltpu.VMEM((3, TOK, WIDE), F32),
            pltpu.VMEM((N_COL, 64, 128), BF16),
            pltpu.SemaphoreType.DMA((8,)),
        ],
        compiler_params=params(56),
        cost_estimate=pl.CostEstimate(flops=2 * TOK * BLOCK * 4 * WIDE, bytes_accessed=12 * MIB, transcendentals=0),
        name="partner_part",
    )(idx, gathered, *halves, rights, own_t, acc)


def merge_kernel(idx, base, *refs):
    blocks, refs = refs[:7], refs[7:]
    lefts, gathered, acc, rr_ref, mag_ref, t_ref, r_ref = refs[:7]
    out, scale_ref, product, raw, comb, left, par, sems, out_sems = refs[7:]
    prompts, _ = block_copies(idx, gathered, par, None, sems.at[9], None)
    prompts.append(pltpu.make_async_copy(acc.at[0], product, sems.at[10]))
    first = []
    for j in range(8):
        for h in range(2):
            zl = idx[PLACE["zl"]] if h == 0 else 1 - idx[PLACE["zl"]]
            c = j // 2 * 4 + zl * 2 + j % 2
            for k in range(2):
                rows = pl.ds((2 * h + k) * 256, 256)
                first.append(pltpu.make_async_copy(lefts.at[j, rows, :], left.at[c, k], sems.at[8]))
    for c in first:
        c.start()
    col = pl.ds(pl.multiple_of(idx[0] * WIDE, WIDE), WIDE)
    pltpu.make_async_copy(base.at[:, col], raw.at[0], sems.at[0]).start()
    for j in range(7):
        pltpu.make_async_copy(blocks[j].at[pl.ds(0, BLOCK), :], raw.at[j + 1], sems.at[j + 1]).start()
    for c in prompts:
        c.start()
    wait_all(first)

    def part(i, squares):
        j, h = i // 2, i % 2

        @pl.when(h == 0)
        def _():
            pltpu.make_async_copy(blocks[0], raw.at[j], sems.at[j]).wait()

        factor = left[pl.ds(h * 8, 8), j % 2, pl.ds(pl.multiple_of(j // 2 * 64, 64), 64), :].reshape(512, 128)
        update = jnp.dot(factor, rr_ref[...], preferred_element_type=F32)
        for c in range(8):
            for k in range(2):
                rows = pl.ds(pl.multiple_of(h * 1024 + c * 128 + k * 64, 64), 64)
                value = raw[j, rows, :].astype(F32) + update[c * 64 : (c + 1) * 64, k * WIDE : (k + 1) * WIDE]
                comb[j, rows, :] = value
                squares += (value * value).reshape(8, 8, WIDE).sum(axis=0)
        return squares

    squares = lax.fori_loop(0, 16, part, jnp.zeros((8, WIDE), F32))
    scale = mag_ref[...] / jnp.sqrt(squares.sum(axis=0, keepdims=True) + 1e-6)
    scale_ref[...] = scale
    wait_all(prompts)
    product[...] += dot(par[...], raw[1]) + dot(t_ref[...], r_ref[...])

    def out_copy(j):
        rows = pl.ds(pl.multiple_of(idx[PLACE["rows"] + j] * BLOCK, BLOCK), BLOCK)
        return pltpu.make_async_copy(raw.at[j], out.at[rows, :], out_sems.at[j])

    @pl.loop(0, 8)
    def _(j):
        @pl.loop(0, 8)
        def _(m):
            rows = pl.ds(pl.multiple_of(m * 256, 256), 256)
            raw[j, rows, :] = (comb[j, rows, :] * scale).astype(BF16)

        out_copy(j).start()

    @pl.loop(0, 8)
    def _(j):
        out_copy(j).wait()


def merge(idx, base, blocks, lefts, gathered, acc, rr, mag, t, right):
    any_space = pl.BlockSpec(memory_space=pltpu.HBM)
    vmem = pl.BlockSpec(memory_space=pltpu.VMEM)
    return pl.pallas_call(
        merge_kernel,
        out_shape=[
            jax.ShapeDtypeStruct((8 * BLOCK, WIDE), BF16),
            jax.ShapeDtypeStruct((1, WIDE), F32),
            jax.ShapeDtypeStruct((TOK, WIDE), F32),
        ],
        in_specs=[pl.BlockSpec(memory_space=pltpu.SMEM)] + [any_space] * 11 + [vmem] * 4,
        out_specs=[any_space, vmem, vmem],
        scratch_shapes=[
            pltpu.VMEM((8, BLOCK, WIDE), BF16),
            pltpu.VMEM((8, BLOCK, WIDE), F32),
            pltpu.VMEM((N_COL, 2, 256, 128), BF16),
            pltpu.VMEM((TOK, BLOCK), BF16),
            pltpu.SemaphoreType.DMA((11,)),
            pltpu.SemaphoreType.DMA((8,)),
        ],
        compiler_params=params(56),
        cost_estimate=pl.CostEstimate(flops=2 * 128 * 512 * 8192, bytes_accessed=18 * MIB, transcendentals=0),
        name="merge",
    )(idx, base, *blocks, lefts, gathered, acc, rr, mag, t, right)


def shards(prompt, base, factor_left, factor_right, magnitude):
    row = lax.axis_index("row").astype(jnp.int32)
    zh, y = row // 4, row % 4
    order = (0,) + SHIFTS

    def served_by(dz, dy):
        return ((zh + dz) % 2) * 4 + (y + dy) % 4

    left = jnp.concatenate([factor_left[:64], factor_left[64:]], axis=1)
    right = factor_right.reshape(8, 16, 128).transpose(1, 0, 2).reshape(128, 128)
    small = jnp.concatenate([prompt, left], axis=0)

    partner, beside, beside_partner = swap(small, 64), swap(small, 2), swap(small, 66)
    relayed = {}
    places = [served_by(0, d) for d in SHIFTS] + [served_by(1, d) for d in SHIFTS + (0,)]
    slices = pack(places, base, 3)
    packed, packed_half = dict(zip(SHIFTS, slices)), dict(zip(SHIFTS + (0,), slices[3:]))

    wave = (partner, beside, beside_partner, packed[2])
    partner, beside, beside_partner, _ = lax.optimization_barrier(wave)
    gathered = gather_x(jnp.concatenate([small, beside], axis=0))
    gathered_partner = gather_x(jnp.concatenate([partner, beside_partner], axis=0))
    half = {d: move(after(packed_half[d], *wave), dz=1) for d in (-1, 1)}
    factors = jnp.concatenate([left, beside[TOK:], right], axis=0)
    straight = {}
    for d, block in zip(SHIFTS, append(left, beside, right, [packed[d] for d in SHIFTS])):
        straight[d] = move(block, dy=d)

    wave = (*(straight[d] for d in SHIFTS), half[-1], half[1])
    for d in (1, -1):
        relayed[d] = move(after(half[d], *wave), dy=d)
    half[2] = move(after(packed_half[2], *wave), dz=1)
    got = [factors]
    for d in SHIFTS:
        below = straight[d][BLOCK:]
        got.append(jnp.concatenate([below[:, :128], below[:, 128:]], axis=0))
    got = jnp.stack(got)
    places = [((zh + k) % 2) * 4 + (y - d) % 4 for d in order for k in range(2)]
    at_col = lax.axis_index("col").astype(jnp.int32)
    idx = jnp.stack([served_by(0, d) for d in order] + places + [at_col // 2 % 2])
    acc, own_t = own_part(idx, after(gathered, *wave), base)
    got_partner = swap(after(got, *wave, own_t), 64)

    wave = (half[2], relayed[1], relayed[-1], own_t)
    half[0] = move(after(packed_half[0], *wave), dz=1)
    relayed[2] = move(after(half[2], *wave), dy=2)
    lefts = jnp.stack([got[:, :64], got_partner[:, :64], got[:, 64:128], got_partner[:, 64:128]]).reshape(1024, 128)
    lefts = gather_x(after(lefts, *wave))

    rights = jnp.stack([jnp.stack([got[j, 128:], got_partner[j, 128:]]) for j in (0, 2, 3, 1)])
    rights = lax.dynamic_slice_in_dim(jnp.concatenate([rights, rights], axis=0), (4 - y) % 4, 4, 0)
    rights = lax.dynamic_slice_in_dim(jnp.concatenate([rights, rights[:, :1]], axis=1), zh, 2, 1)
    rights = rights.reshape(4, 2, 16, 8, 128).transpose(1, 0, 3, 2, 4).reshape(64, 2048)

    *sends, t = partner_part(idx, gathered_partner, [half[d] for d in SHIFTS], rights, own_t, acc)
    sums = [move(s, dy=d) for s, d in zip(sends, SHIFTS)]

    right_mine = lax.dynamic_slice(rights, (0, row * WIDE), (64, WIDE))
    rr = jnp.pad(right_mine, ((0, 64), (0, WIDE))) + jnp.pad(right_mine, ((64, 0), (WIDE, 0)))
    mag = lax.dynamic_slice(magnitude, (row * WIDE,), (WIDE,))[None]
    blocks = [half[0]]
    for d in SHIFTS:
        blocks += [straight[d], relayed[d]]
    serving, scale, product = merge(
        idx, base, blocks, lefts, gathered_partner, acc, rr, mag, t, right_mine
    )

    for s in sums:
        product = product + s.astype(F32)
    return serving[None], (product * scale).astype(BF16)[None]


def solution(mesh):
    in_specs = (
        P(None, ("row", "col")),
        P("row", "col"),
        P(("row", "col"), None),
        P("row", "col"),
        P("col"),
    )
    out_specs = (P("row", None, "col"), P("row", None, "col"))
    return jax.shard_map(shards, mesh=mesh, in_specs=in_specs, out_specs=out_specs, check_vma=False)
```

```python
import functools

import jax
import jax.numpy as jnp
from jax import lax
from jax.experimental import pallas as pl
from jax.experimental.pallas import tpu as pltpu
from jax.sharding import PartitionSpec as P

AXES = ("row", "col")
SHIFTS = (1, -1, 2)
BLOCK = 2048
WIDE = 256
TOK = 1024
N_COL = 16
MIB = 1024 * 1024
F32 = jnp.float32
BF16 = jnp.bfloat16


def move(a, dz=0, dy=0):
    pairs = []
    for r in range(8):
        zh, y = divmod(r, 4)
        to = ((zh + dz) % 2) * 4 + (y + dy) % 4
        pairs += [(r * N_COL + c, to * N_COL + c) for c in range(N_COL)]
    return lax.ppermute(a, AXES, pairs)


def swap(a, bits):
    return lax.ppermute(a, AXES, [(i, i ^ bits) for i in range(128)])


def gather_x(a):
    groups = [[16 * r + 4 * x + 2 * zl + k for x in range(4) for k in range(2)] for r in range(8) for zl in range(2)]
    return lax.all_gather(a, AXES, axis=0, tiled=False, axis_index_groups=groups)


def after(x, *deps):
    return lax.optimization_barrier((x, *deps))[0]


def params(mib, **kw):
    return pltpu.CompilerParams(vmem_limit_bytes=mib * MIB, **kw)


PART = TOK + 64
PLACE = dict(served=0, rows=4, zl=12)


def block_copies(idx, gathered, whole, left, sem, left_sem):
    prompts, lefts = [], []
    for j in range(8):
        for h in range(2):
            zl = idx[PLACE["zl"]] if h == 0 else 1 - idx[PLACE["zl"]]
            c = j // 2 * 4 + zl * 2 + j % 2
            lanes = pl.ds(pl.multiple_of(c * 128, 128), 128)
            prompts.append(pltpu.make_async_copy(gathered.at[j, pl.ds(h * PART, TOK), :], whole.at[:, lanes], sem))
            if left is not None:
                lefts.append(pltpu.make_async_copy(gathered.at[j, pl.ds(h * PART + TOK, 64), :], left.at[c], left_sem))
    return prompts, lefts


EXTRA = 128


def pack_kernel(n, idx, base, *refs):
    outs, (stage, sems) = refs[:-2], refs[-2:]
    reads, writes = [], []
    for j in range(n):
        at = pl.ds(pl.multiple_of(idx[j] * WIDE, WIDE), WIDE)
        for h in range(2):
            rows = pl.ds(h * 1024, 1024)
            reads.append(pltpu.make_async_copy(base.at[rows, at], stage.at[j, rows, :], sems.at[0, j, h]))
            writes.append(pltpu.make_async_copy(stage.at[j, rows, :], outs[j].at[rows, :], sems.at[1, j, h]))
    for c in reads:
        c.start()
    for r, w in zip(reads, writes):
        r.wait()
        w.start()
    wait_all(writes)


def pack(places, base, extra):
    n = len(places)
    return pl.pallas_call(
        functools.partial(pack_kernel, n),
        out_shape=[jax.ShapeDtypeStruct((BLOCK + EXTRA * (j < extra), WIDE), BF16) for j in range(n)],
        in_specs=specs("sh"),
        out_specs=specs("h" * n),
        scratch_shapes=[pltpu.VMEM((n, BLOCK, WIDE), BF16), pltpu.SemaphoreType.DMA((2, n, 2))],
        compiler_params=params(56),
        cost_estimate=pl.CostEstimate(flops=0, bytes_accessed=2 * n * MIB, transcendentals=0),
        name="pack",
    )(jnp.stack(places), base)


def join_kernel(left, right, small, beside, partner, beside_partner, a1, a2, a3, o1, o2, o3, own, par, sem):
    copies = []
    for out, parts in ((own, (small, beside)), (par, (partner, beside_partner))):
        for h in range(2):
            copies.append(pltpu.make_async_copy(parts[h], out.at[pl.ds(h * PART, PART), :], sem))
    for o in (o1, o2, o3):
        for src, row, lane in ((left, 0, 0), (beside.at[pl.ds(TOK, 64), :], 64, 0), (right, 0, 128)):
            dst = o.at[pl.ds(BLOCK + row, src.shape[0]), pl.ds(lane, 128)]
            copies.append(pltpu.make_async_copy(src, dst, sem))
    for c in copies:
        c.start()
    wait_all(copies)


def join(left, right, small, beside, partner, beside_partner, blocks):
    pair = jax.ShapeDtypeStruct((2 * PART, 128), BF16)
    return pl.pallas_call(
        join_kernel,
        out_shape=[jax.ShapeDtypeStruct(b.shape, b.dtype) for b in blocks] + [pair, pair],
        in_specs=specs("vvvvvvhhh"),
        out_specs=specs("hhhhh"),
        scratch_shapes=[pltpu.SemaphoreType.DMA],
        input_output_aliases={6: 0, 7: 1, 8: 2},
        compiler_params=params(56),
        cost_estimate=pl.CostEstimate(flops=0, bytes_accessed=3 * MIB, transcendentals=0),
        name="join",
    )(left, right, small, beside, partner, beside_partner, *blocks)


def wait_all(copies):
    for c in copies:
        c.wait()


def specs(kinds):
    space = dict(h=pltpu.HBM, s=pltpu.SMEM, v=pltpu.VMEM)
    return [pl.BlockSpec(memory_space=space[k]) for k in kinds]


def dot(a, b):
    return jnp.dot(a, b, preferred_element_type=F32)


def unpacked(ref):
    value = ref[...]
    return jnp.concatenate([value[:, :, :64], value[:, :, 64:]], axis=1).reshape(BLOCK, 64)


def own_kernel(idx, gathered, base, acc, t_ref, own, w, left, sems):
    prompts, lefts = block_copies(idx, gathered, own, left, sems.at[4], sems.at[5])
    cols = []
    for j in range(4):
        at = pl.ds(pl.multiple_of(idx[j] * WIDE, WIDE), WIDE)
        cols.append(pltpu.make_async_copy(base.at[:, at], w.at[j], sems.at[j]))
    for c in lefts + prompts + cols:
        c.start()
    wait_all(lefts)
    factor = unpacked(left)
    wait_all(prompts)
    t_ref[...] = dot(own[...], factor)
    for j in range(4):
        cols[j].wait()
        acc[j] = dot(own[...], w[j])


def own_part(idx, gathered, base):
    return pl.pallas_call(
        own_kernel,
        out_shape=[jax.ShapeDtypeStruct((4, TOK, WIDE), F32), jax.ShapeDtypeStruct((TOK, 64), F32)],
        in_specs=specs("shh"),
        out_specs=specs("vv"),
        scratch_shapes=[
            pltpu.VMEM((TOK, BLOCK), BF16),
            pltpu.VMEM((4, BLOCK, WIDE), BF16),
            pltpu.VMEM((N_COL, 64, 128), BF16),
            pltpu.SemaphoreType.DMA((6,)),
        ],
        compiler_params=params(56),
        cost_estimate=pl.CostEstimate(flops=2 * TOK * BLOCK * 5 * WIDE, bytes_accessed=13 * MIB, transcendentals=0),
        name="own_part",
    )(idx, gathered, base)


def partner_kernel(idx, gathered, h1, h2, h3, r_ref, own_t, acc, o1, o2, o3, t_ref, par, w, part, left, sems):
    prompts, lefts = block_copies(idx, gathered, par, left, sems.at[6], sems.at[7])
    halves = [pltpu.make_async_copy(h, w.at[i], sems.at[i]) for i, h in enumerate((h1, h2, h3))]
    parts = [pltpu.make_async_copy(acc.at[i + 1], part.at[i], sems.at[3 + i]) for i in range(3)]
    for c in lefts + prompts:
        c.start()
    for h, p in zip(halves, parts):
        h.start()
        p.start()
    wait_all(lefts)
    factor = unpacked(left)
    wait_all(prompts)
    t = (own_t[...] + dot(par[...], factor)).astype(BF16)
    t_ref[...] = t
    for i, o in enumerate((o1, o2, o3)):
        right = r_ref[:, pl.ds(pl.multiple_of(idx[1 + i] % 4 * WIDE, WIDE), WIDE)]
        halves[i].wait()
        parts[i].wait()
        o[...] = (dot(par[...], w[i]) + dot(t, right) + part[i]).astype(BF16)


def partner_part(idx, gathered, halves, rights, own_t, acc):
    send = jax.ShapeDtypeStruct((TOK, WIDE), BF16)
    return pl.pallas_call(
        partner_kernel,
        out_shape=[send, send, send, jax.ShapeDtypeStruct((TOK, 64), BF16)],
        in_specs=specs("shhhhvvh"),
        out_specs=specs("vvvv"),
        scratch_shapes=[
            pltpu.VMEM((TOK, BLOCK), BF16),
            pltpu.VMEM((3, BLOCK, WIDE), BF16),
            pltpu.VMEM((3, TOK, WIDE), F32),
            pltpu.VMEM((N_COL, 64, 128), BF16),
            pltpu.SemaphoreType.DMA((8,)),
        ],
        compiler_params=params(56),
        cost_estimate=pl.CostEstimate(flops=2 * TOK * BLOCK * 4 * WIDE, bytes_accessed=12 * MIB, transcendentals=0),
        name="partner_part",
    )(idx, gathered, *halves, rights, own_t, acc)


def merge_kernel(idx, base, *refs):
    blocks, refs = refs[:7], refs[7:]
    lefts, gathered, acc, rr_ref, mag_ref, t_ref, r_ref = refs[:7]
    out, scale_ref, product, raw, comb, left, par, sems, out_sems = refs[7:]
    prompts, _ = block_copies(idx, gathered, par, None, sems.at[9], None)
    prompts.append(pltpu.make_async_copy(acc.at[0], product, sems.at[10]))
    first = []
    for j in range(8):
        for h in range(2):
            zl = idx[PLACE["zl"]] if h == 0 else 1 - idx[PLACE["zl"]]
            c = j // 2 * 4 + zl * 2 + j % 2
            for k in range(2):
                rows = pl.ds((2 * h + k) * 256, 256)
                first.append(pltpu.make_async_copy(lefts.at[j, rows, :], left.at[c, k], sems.at[8]))
    for c in first:
        c.start()
    col = pl.ds(pl.multiple_of(idx[0] * WIDE, WIDE), WIDE)
    pltpu.make_async_copy(base.at[:, col], raw.at[0], sems.at[0]).start()
    for j in range(7):
        pltpu.make_async_copy(blocks[j].at[pl.ds(0, BLOCK), :], raw.at[j + 1], sems.at[j + 1]).start()
    for c in prompts:
        c.start()
    wait_all(first)

    def part(i, squares):
        j, h = i // 2, i % 2

        @pl.when(h == 0)
        def _():
            pltpu.make_async_copy(blocks[0], raw.at[j], sems.at[j]).wait()

        factor = left[pl.ds(h * 8, 8), j % 2, pl.ds(pl.multiple_of(j // 2 * 64, 64), 64), :].reshape(512, 128)
        update = jnp.dot(factor, rr_ref[...], preferred_element_type=F32)
        for c in range(8):
            for k in range(2):
                rows = pl.ds(pl.multiple_of(h * 1024 + c * 128 + k * 64, 64), 64)
                value = raw[j, rows, :].astype(F32) + update[c * 64 : (c + 1) * 64, k * WIDE : (k + 1) * WIDE]
                comb[j, rows, :] = value
                squares += (value * value).reshape(8, 8, WIDE).sum(axis=0)
        return squares

    squares = lax.fori_loop(0, 16, part, jnp.zeros((8, WIDE), F32))
    scale = mag_ref[...] / jnp.sqrt(squares.sum(axis=0, keepdims=True) + 1e-6)
    scale_ref[...] = scale
    wait_all(prompts)
    product[...] += dot(par[...], raw[1]) + dot(t_ref[...], r_ref[...])

    def out_copy(j):
        rows = pl.ds(pl.multiple_of(idx[PLACE["rows"] + j] * BLOCK, BLOCK), BLOCK)
        return pltpu.make_async_copy(raw.at[j], out.at[rows, :], out_sems.at[j])

    @pl.loop(0, 8)
    def _(j):
        @pl.loop(0, 8)
        def _(m):
            rows = pl.ds(pl.multiple_of(m * 256, 256), 256)
            raw[j, rows, :] = (comb[j, rows, :] * scale).astype(BF16)

        out_copy(j).start()

    @pl.loop(0, 8)
    def _(j):
        out_copy(j).wait()


def merge(idx, base, blocks, lefts, gathered, acc, rr, mag, t, right):
    any_space = pl.BlockSpec(memory_space=pltpu.HBM)
    vmem = pl.BlockSpec(memory_space=pltpu.VMEM)
    return pl.pallas_call(
        merge_kernel,
        out_shape=[
            jax.ShapeDtypeStruct((8 * BLOCK, WIDE), BF16),
            jax.ShapeDtypeStruct((1, WIDE), F32),
            jax.ShapeDtypeStruct((TOK, WIDE), F32),
        ],
        in_specs=[pl.BlockSpec(memory_space=pltpu.SMEM)] + [any_space] * 11 + [vmem] * 4,
        out_specs=[any_space, vmem, vmem],
        scratch_shapes=[
            pltpu.VMEM((8, BLOCK, WIDE), BF16),
            pltpu.VMEM((8, BLOCK, WIDE), F32),
            pltpu.VMEM((N_COL, 2, 256, 128), BF16),
            pltpu.VMEM((TOK, BLOCK), BF16),
            pltpu.SemaphoreType.DMA((11,)),
            pltpu.SemaphoreType.DMA((8,)),
        ],
        compiler_params=params(56),
        cost_estimate=pl.CostEstimate(flops=2 * 128 * 512 * 8192, bytes_accessed=18 * MIB, transcendentals=0),
        name="merge",
    )(idx, base, *blocks, lefts, gathered, acc, rr, mag, t, right)


def shards(prompt, base, factor_left, factor_right, magnitude):
    row = lax.axis_index("row").astype(jnp.int32)
    zh, y = row // 4, row % 4
    order = (0,) + SHIFTS

    def served_by(dz, dy):
        return ((zh + dz) % 2) * 4 + (y + dy) % 4

    left = jnp.concatenate([factor_left[:64], factor_left[64:]], axis=1)
    small = jnp.concatenate([prompt, left], axis=0)
    right = factor_right.reshape(8, 16, 128).transpose(1, 0, 2).reshape(128, 128)

    partner, beside, beside_partner = swap(small, 64), swap(small, 2), swap(small, 66)
    relayed = {}
    places = [served_by(0, d) for d in SHIFTS] + [served_by(1, d) for d in SHIFTS + (0,)]
    slices = pack(places, base, 3)
    packed, packed_half = dict(zip(SHIFTS, slices)), dict(zip(SHIFTS + (0,), slices[3:]))

    wave = (partner, beside, beside_partner, packed[2])
    partner, beside, beside_partner, _ = lax.optimization_barrier(wave)
    half = {d: move(after(packed_half[d], *wave), dz=1) for d in (-1, 1)}
    *blocks, prompts, prompts_partner = join(
        left, right, small, beside, partner, beside_partner, [packed[d] for d in SHIFTS]
    )
    gathered, gathered_partner = gather_x(prompts), gather_x(prompts_partner)
    straight = {d: move(block, dy=d) for d, block in zip(SHIFTS, blocks)}

    wave = (half[-1], half[1])
    for d in (1, -1):
        relayed[d] = move(after(half[d], *wave), dy=d)
    half[2] = move(after(packed_half[2], *wave), dz=1)
    got = [jnp.concatenate([left, beside[TOK:], right], axis=0)]
    for d in SHIFTS:
        below = straight[d][BLOCK:]
        got.append(jnp.concatenate([below[:, :128], below[:, 128:]], axis=0))
    got = jnp.stack(got)
    places = [((zh + k) % 2) * 4 + (y - d) % 4 for d in order for k in range(2)]
    at_col = lax.axis_index("col").astype(jnp.int32)
    idx = jnp.stack([served_by(0, d) for d in order] + places + [at_col // 2 % 2])
    acc, own_t = own_part(idx, after(gathered, *wave), base)
    def rights_for(half_of_row):
        return lax.dynamic_slice_in_dim(got, 128 + half_of_row * 64, 64, 1)

    to_partner = jnp.concatenate([got[:, :128], rights_for(1 - zh)], axis=1)
    got_partner = swap(after(to_partner, *wave, own_t), 64)

    wave = (half[2], relayed[1], relayed[-1], own_t)
    half[0] = move(after(packed_half[0], *wave), dz=1)
    relayed[2] = move(after(half[2], *wave), dy=2)
    lefts = jnp.stack([got[:, :64], got_partner[:, :64], got[:, 64:128], got_partner[:, 64:128]]).reshape(1024, 128)
    lefts = gather_x(after(lefts, *wave))

    rights = jnp.stack([jnp.stack([rights_for(zh)[j], got_partner[j, 128:]]) for j in (0, 2, 3, 1)])
    rights = lax.dynamic_slice_in_dim(jnp.concatenate([rights, rights], axis=0), (4 - y) % 4, 4, 0)
    rights = lax.dynamic_slice_in_dim(jnp.concatenate([rights, rights[:, :1]], axis=1), zh, 2, 1)
    rights = rights.reshape(4, 2, 8, 8, 128).transpose(1, 0, 3, 2, 4).reshape(64, 1024)

    *sends, t = partner_part(idx, gathered_partner, [half[d] for d in SHIFTS], rights, own_t, acc)
    sums = [move(s, dy=d) for s, d in zip(sends, SHIFTS)]

    right_mine = lax.dynamic_slice(rights, (0, y * WIDE), (64, WIDE))
    rr = jnp.pad(right_mine, ((0, 64), (0, WIDE))) + jnp.pad(right_mine, ((64, 0), (WIDE, 0)))
    mag = lax.dynamic_slice(magnitude, (row * WIDE,), (WIDE,))[None]
    blocks = [half[0]]
    for d in SHIFTS:
        blocks += [straight[d], relayed[d]]
    serving, scale, product = merge(
        idx, base, blocks, lefts, gathered_partner, acc, rr, mag, t, right_mine
    )

    product = lax.optimization_barrier(product + sums[0].astype(F32) + sums[1].astype(F32)) + sums[2].astype(F32)
    return serving[None], (product * scale).astype(BF16)[None]


def solution(mesh):
    in_specs = (
        P(None, ("row", "col")),
        P("row", "col"),
        P(("row", "col"), None),
        P("row", "col"),
        P("col"),
    )
    out_specs = (P("row", None, "col"), P("row", None, "col"))
    return jax.shard_map(shards, mesh=mesh, in_specs=in_specs, out_specs=out_specs, check_vma=False)
```

```python
import functools

import jax
import jax.numpy as jnp
from jax import lax
from jax.experimental import pallas as pl
from jax.experimental.pallas import tpu as pltpu
from jax.sharding import PartitionSpec as P

AXES = ("row", "col")
SHIFTS = (1, -1, 2)
BLOCK = 2048
WIDE = 256
TOK = 1024
N_COL = 16
MIB = 1024 * 1024
F32 = jnp.float32
BF16 = jnp.bfloat16


def move(a, dz=0, dy=0):
    pairs = []
    for r in range(8):
        zh, y = divmod(r, 4)
        to = ((zh + dz) % 2) * 4 + (y + dy) % 4
        pairs += [(r * N_COL + c, to * N_COL + c) for c in range(N_COL)]
    return lax.ppermute(a, AXES, pairs)


def swap(a, bits):
    return lax.ppermute(a, AXES, [(i, i ^ bits) for i in range(128)])


def gather_x(a):
    groups = [[16 * r + 4 * x + 2 * zl + k for x in range(4) for k in range(2)] for r in range(8) for zl in range(2)]
    return lax.all_gather(a, AXES, axis=0, tiled=False, axis_index_groups=groups)


def after(x, *deps):
    return lax.optimization_barrier((x, *deps))[0]


def params(mib, **kw):
    return pltpu.CompilerParams(vmem_limit_bytes=mib * MIB, **kw)


PART = TOK + 64
PLACE = dict(served=0, rows=4, zl=12)


def block_copies(idx, gathered, whole, left, sem, left_sem):
    prompts, lefts = [], []
    for j in range(8):
        for h in range(2):
            zl = idx[PLACE["zl"]] if h == 0 else 1 - idx[PLACE["zl"]]
            c = j // 2 * 4 + zl * 2 + j % 2
            lanes = pl.ds(pl.multiple_of(c * 128, 128), 128)
            prompts.append(pltpu.make_async_copy(gathered.at[j, pl.ds(h * PART, TOK), :], whole.at[:, lanes], sem))
            if left is not None:
                lefts.append(pltpu.make_async_copy(gathered.at[j, pl.ds(h * PART + TOK, 64), :], left.at[c], left_sem))
    return prompts, lefts


EXTRA = 128


def pack_kernel(n, idx, base, *refs):
    outs, (stage, sems) = refs[:-2], refs[-2:]
    reads, writes = [], []
    for j in range(n):
        at = pl.ds(pl.multiple_of(idx[j] * WIDE, WIDE), WIDE)
        for h in range(2):
            rows = pl.ds(h * 1024, 1024)
            reads.append(pltpu.make_async_copy(base.at[rows, at], stage.at[j, rows, :], sems.at[0, j, h]))
            writes.append(pltpu.make_async_copy(stage.at[j, rows, :], outs[j].at[rows, :], sems.at[1, j, h]))
    for c in reads:
        c.start()
    for r, w in zip(reads, writes):
        r.wait()
        w.start()
    wait_all(writes)


def pack(places, base, extra):
    n = len(places)
    return pl.pallas_call(
        functools.partial(pack_kernel, n),
        out_shape=[jax.ShapeDtypeStruct((BLOCK + e, WIDE), BF16) for e in extra],
        in_specs=specs("sh"),
        out_specs=specs("h" * n),
        scratch_shapes=[pltpu.VMEM((n, BLOCK, WIDE), BF16), pltpu.SemaphoreType.DMA((2, n, 2))],
        compiler_params=params(56),
        cost_estimate=pl.CostEstimate(flops=0, bytes_accessed=2 * n * MIB, transcendentals=0),
        name="pack",
    )(jnp.stack(places), base)


def join_kernel(left, right, small, beside, partner, beside_partner, a1, a2, a3, o1, o2, o3, own, par, sem):
    copies = []
    for out, parts in ((own, (small, beside)), (par, (partner, beside_partner))):
        for h in range(2):
            copies.append(pltpu.make_async_copy(parts[h], out.at[pl.ds(h * PART, PART), :], sem))
    for o in (o1, o2, o3):
        for src, row, lane in ((left, 0, 0), (beside.at[pl.ds(TOK, 64), :], 64, 0), (right, 0, 128)):
            dst = o.at[pl.ds(BLOCK + row, src.shape[0]), pl.ds(lane, 128)]
            copies.append(pltpu.make_async_copy(src, dst, sem))
    for c in copies:
        c.start()
    wait_all(copies)


def join(left, right, small, beside, partner, beside_partner, blocks):
    pair = jax.ShapeDtypeStruct((2 * PART, 128), BF16)
    return pl.pallas_call(
        join_kernel,
        out_shape=[jax.ShapeDtypeStruct(b.shape, b.dtype) for b in blocks] + [pair, pair],
        in_specs=specs("vvvvvvhhh"),
        out_specs=specs("hhhhh"),
        scratch_shapes=[pltpu.SemaphoreType.DMA],
        input_output_aliases={6: 0, 7: 1, 8: 2},
        compiler_params=params(56),
        cost_estimate=pl.CostEstimate(flops=0, bytes_accessed=3 * MIB, transcendentals=0),
        name="join",
    )(left, right, small, beside, partner, beside_partner, *blocks)


def wait_all(copies):
    for c in copies:
        c.wait()


def specs(kinds):
    space = dict(h=pltpu.HBM, s=pltpu.SMEM, v=pltpu.VMEM)
    return [pl.BlockSpec(memory_space=space[k]) for k in kinds]


def dot(a, b):
    return jnp.dot(a, b, preferred_element_type=F32)


def unpacked(ref):
    value = ref[...]
    return jnp.concatenate([value[:, :, :64], value[:, :, 64:]], axis=1).reshape(BLOCK, 64)


def own_kernel(idx, gathered, base, acc, t_ref, own, w, left, sems):
    prompts, lefts = block_copies(idx, gathered, own, left, sems.at[4], sems.at[5])
    cols = []
    for j in range(4):
        at = pl.ds(pl.multiple_of(idx[j] * WIDE, WIDE), WIDE)
        cols.append(pltpu.make_async_copy(base.at[:, at], w.at[j], sems.at[j]))
    for c in lefts + prompts + cols:
        c.start()
    wait_all(lefts)
    factor = unpacked(left)
    wait_all(prompts)
    t_ref[...] = dot(own[...], factor)
    for j in range(4):
        cols[j].wait()
        acc[j] = dot(own[...], w[j])


def own_part(idx, gathered, base):
    return pl.pallas_call(
        own_kernel,
        out_shape=[jax.ShapeDtypeStruct((4, TOK, WIDE), F32), jax.ShapeDtypeStruct((TOK, 64), F32)],
        in_specs=specs("shh"),
        out_specs=specs("vv"),
        scratch_shapes=[
            pltpu.VMEM((TOK, BLOCK), BF16),
            pltpu.VMEM((4, BLOCK, WIDE), BF16),
            pltpu.VMEM((N_COL, 64, 128), BF16),
            pltpu.SemaphoreType.DMA((6,)),
        ],
        compiler_params=params(56),
        cost_estimate=pl.CostEstimate(flops=2 * TOK * BLOCK * 5 * WIDE, bytes_accessed=13 * MIB, transcendentals=0),
        name="own_part",
    )(idx, gathered, base)


def partner_kernel(idx, gathered, h1, h2, h3, r_ref, own_t, acc, o1, o2, o3, t_ref, par, w, part, left, sems):
    prompts, lefts = block_copies(idx, gathered, par, left, sems.at[6], sems.at[7])
    halves = [pltpu.make_async_copy(h, w.at[i], sems.at[i]) for i, h in enumerate((h1, h2, h3))]
    parts = [pltpu.make_async_copy(acc.at[i + 1], part.at[i], sems.at[3 + i]) for i in range(3)]
    for c in lefts + prompts:
        c.start()
    for h, p in zip(halves, parts):
        h.start()
        p.start()
    wait_all(lefts)
    factor = unpacked(left)
    wait_all(prompts)
    t = (own_t[...] + dot(par[...], factor)).astype(BF16)
    t_ref[...] = t
    for i, o in enumerate((o1, o2, o3)):
        right = r_ref[:, pl.ds(pl.multiple_of(idx[1 + i] % 4 * WIDE, WIDE), WIDE)]
        halves[i].wait()
        parts[i].wait()
        o[...] = (dot(par[...], w[i]) + dot(t, right) + part[i]).astype(BF16)


def partner_part(idx, gathered, halves, rights, own_t, acc):
    send = jax.ShapeDtypeStruct((TOK, WIDE), BF16)
    return pl.pallas_call(
        partner_kernel,
        out_shape=[send, send, send, jax.ShapeDtypeStruct((TOK, 64), BF16)],
        in_specs=specs("shhhhvvh"),
        out_specs=specs("vvvv"),
        scratch_shapes=[
            pltpu.VMEM((TOK, BLOCK), BF16),
            pltpu.VMEM((3, BLOCK, WIDE), BF16),
            pltpu.VMEM((3, TOK, WIDE), F32),
            pltpu.VMEM((N_COL, 64, 128), BF16),
            pltpu.SemaphoreType.DMA((8,)),
        ],
        compiler_params=params(56),
        cost_estimate=pl.CostEstimate(flops=2 * TOK * BLOCK * 4 * WIDE, bytes_accessed=12 * MIB, transcendentals=0),
        name="partner_part",
    )(idx, gathered, *halves, rights, own_t, acc)


def merge_kernel(idx, base, *refs):
    blocks, refs = refs[:7], refs[7:]
    lefts, gathered, acc, rr_ref, mag_ref, t_ref, r_ref = refs[:7]
    out, scale_ref, product, raw, comb, left, par, sems, out_sems = refs[7:]
    prompts, _ = block_copies(idx, gathered, par, None, sems.at[9], None)
    prompts.append(pltpu.make_async_copy(acc.at[0], product, sems.at[10]))
    first = []
    for j in range(8):
        for h in range(2):
            zl = idx[PLACE["zl"]] if h == 0 else 1 - idx[PLACE["zl"]]
            c = j // 2 * 4 + zl * 2 + j % 2
            for k in range(2):
                rows = pl.ds((2 * h + k) * 256, 256)
                first.append(pltpu.make_async_copy(lefts.at[j, rows, :], left.at[c, k], sems.at[8]))
    for c in first:
        c.start()
    col = pl.ds(pl.multiple_of(idx[0] * WIDE, WIDE), WIDE)
    pltpu.make_async_copy(base.at[:, col], raw.at[0], sems.at[0]).start()
    for j in range(7):
        pltpu.make_async_copy(blocks[j].at[pl.ds(0, BLOCK), :], raw.at[j + 1], sems.at[j + 1]).start()
    for c in prompts:
        c.start()
    wait_all(first)

    def part(i, squares):
        j, h = i // 2, i % 2

        @pl.when(h == 0)
        def _():
            pltpu.make_async_copy(blocks[0], raw.at[j], sems.at[j]).wait()

        factor = left[pl.ds(h * 8, 8), j % 2, pl.ds(pl.multiple_of(j // 2 * 64, 64), 64), :].reshape(512, 128)
        update = jnp.dot(factor, rr_ref[...], preferred_element_type=F32)
        for c in range(8):
            for k in range(2):
                rows = pl.ds(pl.multiple_of(h * 1024 + c * 128 + k * 64, 64), 64)
                value = raw[j, rows, :].astype(F32) + update[c * 64 : (c + 1) * 64, k * WIDE : (k + 1) * WIDE]
                comb[j, rows, :] = value
                squares += (value * value).reshape(8, 8, WIDE).sum(axis=0)
        return squares

    squares = lax.fori_loop(0, 16, part, jnp.zeros((8, WIDE), F32))
    scale = mag_ref[...] / jnp.sqrt(squares.sum(axis=0, keepdims=True) + 1e-6)
    scale_ref[...] = scale
    wait_all(prompts)
    product[...] += dot(par[...], raw[1]) + dot(t_ref[...], r_ref[...])

    def out_copy(j):
        rows = pl.ds(pl.multiple_of(idx[PLACE["rows"] + j] * BLOCK, BLOCK), BLOCK)
        return pltpu.make_async_copy(raw.at[j], out.at[rows, :], out_sems.at[j])

    @pl.loop(0, 8)
    def _(j):
        @pl.loop(0, 8)
        def _(m):
            rows = pl.ds(pl.multiple_of(m * 256, 256), 256)
            raw[j, rows, :] = (comb[j, rows, :] * scale).astype(BF16)

        out_copy(j).start()

    @pl.loop(0, 8)
    def _(j):
        out_copy(j).wait()


def merge(idx, base, blocks, lefts, gathered, acc, rr, mag, t, right):
    any_space = pl.BlockSpec(memory_space=pltpu.HBM)
    vmem = pl.BlockSpec(memory_space=pltpu.VMEM)
    return pl.pallas_call(
        merge_kernel,
        out_shape=[
            jax.ShapeDtypeStruct((8 * BLOCK, WIDE), BF16),
            jax.ShapeDtypeStruct((1, WIDE), F32),
            jax.ShapeDtypeStruct((TOK, WIDE), F32),
        ],
        in_specs=[pl.BlockSpec(memory_space=pltpu.SMEM)] + [any_space] * 11 + [vmem] * 4,
        out_specs=[any_space, vmem, vmem],
        scratch_shapes=[
            pltpu.VMEM((8, BLOCK, WIDE), BF16),
            pltpu.VMEM((8, BLOCK, WIDE), F32),
            pltpu.VMEM((N_COL, 2, 256, 128), BF16),
            pltpu.VMEM((TOK, BLOCK), BF16),
            pltpu.SemaphoreType.DMA((11,)),
            pltpu.SemaphoreType.DMA((8,)),
        ],
        compiler_params=params(56),
        cost_estimate=pl.CostEstimate(flops=2 * 128 * 512 * 8192, bytes_accessed=18 * MIB, transcendentals=0),
        name="merge",
    )(idx, base, *blocks, lefts, gathered, acc, rr, mag, t, right)


def shards(prompt, base, factor_left, factor_right, magnitude):
    row = lax.axis_index("row").astype(jnp.int32)
    zh, y = row // 4, row % 4
    order = (0,) + SHIFTS

    def served_by(dz, dy):
        return ((zh + dz) % 2) * 4 + (y + dy) % 4

    left = jnp.concatenate([factor_left[:64], factor_left[64:]], axis=1)
    small = jnp.concatenate([prompt, left], axis=0)
    right = factor_right.reshape(8, 16, 128).transpose(1, 0, 2).reshape(128, 128)

    partner, beside, beside_partner = swap(small, 64), swap(small, 2), swap(small, 66)
    relayed = {}
    places = [served_by(0, d) for d in SHIFTS] + [served_by(1, d) for d in SHIFTS + (0,)]
    slices = pack(places, base, (EXTRA, EXTRA, EXTRA + 64) + (0,) * 3 + (16,))
    packed, packed_half = dict(zip(SHIFTS, slices)), dict(zip(SHIFTS + (0,), slices[3:]))

    wave = (partner, beside, beside_partner, packed[2])
    partner, beside, beside_partner, _ = lax.optimization_barrier(wave)
    half = {d: move(after(packed_half[d], *wave), dz=1) for d in (-1, 1)}
    *blocks, prompts, prompts_partner = join(
        left, right, small, beside, partner, beside_partner, [packed[d] for d in SHIFTS]
    )
    gathered, gathered_partner = gather_x(prompts), gather_x(prompts_partner)
    straight = {d: move(block, dy=d) for d, block in zip(SHIFTS, blocks)}

    wave = (half[-1], half[1])
    for d in (1, -1):
        relayed[d] = move(after(half[d], *wave), dy=d)
    half[2] = move(after(packed_half[2], *wave), dz=1)
    got = [jnp.concatenate([left, beside[TOK:], right], axis=0)]
    for d in SHIFTS:
        below = straight[d][BLOCK : BLOCK + EXTRA]
        got.append(jnp.concatenate([below[:, :128], below[:, 128:]], axis=0))
    got = jnp.stack(got)
    places = [((zh + k) % 2) * 4 + (y - d) % 4 for d in order for k in range(2)]
    at_col = lax.axis_index("col").astype(jnp.int32)
    idx = jnp.stack([served_by(0, d) for d in order] + places + [at_col // 2 % 2])
    acc, own_t = own_part(idx, after(gathered, *wave), base)
    def rights_for(half_of_row):
        return lax.dynamic_slice_in_dim(got, 128 + half_of_row * 64, 64, 1)

    to_partner = jnp.concatenate([got[:, :128], rights_for(1 - zh)], axis=1)
    got_partner = swap(after(to_partner, *wave, own_t), 64)

    wave = (half[2], relayed[1], relayed[-1], own_t)
    half[0] = move(after(packed_half[0], *wave), dz=1)
    relayed[2] = move(after(half[2], *wave), dy=2)
    lefts = jnp.stack([got[:, :64], got_partner[:, :64], got[:, 64:128], got_partner[:, 64:128]]).reshape(1024, 128)
    lefts = gather_x(after(lefts, *wave))

    rights = jnp.stack([jnp.stack([rights_for(zh)[j], got_partner[j, 128:]]) for j in (0, 2, 3, 1)])
    rights = lax.dynamic_slice_in_dim(jnp.concatenate([rights, rights], axis=0), (4 - y) % 4, 4, 0)
    rights = lax.dynamic_slice_in_dim(jnp.concatenate([rights, rights[:, :1]], axis=1), zh, 2, 1)
    rights = rights.reshape(4, 2, 8, 8, 128).transpose(1, 0, 3, 2, 4).reshape(64, 1024)

    *sends, t = partner_part(idx, gathered_partner, [half[d] for d in SHIFTS], rights, own_t, acc)
    sums = [move(s, dy=d) for s, d in zip(sends, SHIFTS)]

    right_mine = lax.dynamic_slice(rights, (0, y * WIDE), (64, WIDE))
    rr = jnp.pad(right_mine, ((0, 64), (0, WIDE))) + jnp.pad(right_mine, ((64, 0), (WIDE, 0)))
    mag = lax.dynamic_slice(magnitude, (row * WIDE,), (WIDE,))[None]
    blocks = [half[0]]
    for d in SHIFTS:
        blocks += [straight[d], relayed[d]]
    serving, scale, product = merge(
        idx, base, blocks, lefts, gathered_partner, acc, rr, mag, t, right_mine
    )

    product = lax.optimization_barrier(product + sums[0].astype(F32) + sums[1].astype(F32)) + sums[2].astype(F32)
    return serving[None], (product * scale).astype(BF16)[None]


def solution(mesh):
    in_specs = (
        P(None, ("row", "col")),
        P("row", "col"),
        P(("row", "col"), None),
        P("row", "col"),
        P("col"),
    )
    out_specs = (P("row", None, "col"), P("row", None, "col"))
    return jax.shard_map(shards, mesh=mesh, in_specs=in_specs, out_specs=out_specs, check_vma=False)
```

```python
import functools

import jax
import jax.numpy as jnp
from jax import lax
from jax.experimental import pallas as pl
from jax.experimental.pallas import tpu as pltpu
from jax.sharding import PartitionSpec as P

AXES = ("row", "col")
SHIFTS = (1, -1, 2)
BLOCK = 2048
WIDE = 256
TOK = 1024
N_COL = 16
MIB = 1024 * 1024
F32 = jnp.float32
BF16 = jnp.bfloat16


def move(a, dz=0, dy=0):
    pairs = []
    for r in range(8):
        zh, y = divmod(r, 4)
        to = ((zh + dz) % 2) * 4 + (y + dy) % 4
        pairs += [(r * N_COL + c, to * N_COL + c) for c in range(N_COL)]
    return lax.ppermute(a, AXES, pairs)


def swap(a, bits):
    return lax.ppermute(a, AXES, [(i, i ^ bits) for i in range(128)])


def gather_x(a):
    groups = [[16 * r + 4 * x + 2 * zl + k for x in range(4) for k in range(2)] for r in range(8) for zl in range(2)]
    return lax.all_gather(a, AXES, axis=0, tiled=False, axis_index_groups=groups)


def after(x, *deps):
    return lax.optimization_barrier((x, *deps))[0]


def params(mib, **kw):
    return pltpu.CompilerParams(vmem_limit_bytes=mib * MIB, **kw)


PART = TOK + 64
PLACE = dict(served=0, rows=4, zl=12)


def block_copies(idx, gathered, whole, left, sem, left_sem):
    prompts, lefts = [], []
    for j in range(8):
        for h in range(2):
            zl = idx[PLACE["zl"]] if h == 0 else 1 - idx[PLACE["zl"]]
            c = j // 2 * 4 + zl * 2 + j % 2
            lanes = pl.ds(pl.multiple_of(c * 128, 128), 128)
            prompts.append(pltpu.make_async_copy(gathered.at[j, pl.ds(h * PART, TOK), :], whole.at[:, lanes], sem))
            if left is not None:
                lefts.append(pltpu.make_async_copy(gathered.at[j, pl.ds(h * PART + TOK, 64), :], left.at[c], left_sem))
    return prompts, lefts


EXTRA = 128


def pack_kernel(n, idx, base, *refs):
    outs, (stage, sems) = refs[:-2], refs[-2:]
    reads, writes = [], []
    for j in range(n):
        at = pl.ds(pl.multiple_of(idx[j] * WIDE, WIDE), WIDE)
        for h in range(2):
            rows = pl.ds(h * 1024, 1024)
            reads.append(pltpu.make_async_copy(base.at[rows, at], stage.at[j, rows, :], sems.at[0, j, h]))
            writes.append(pltpu.make_async_copy(stage.at[j, rows, :], outs[j].at[rows, :], sems.at[1, j, h]))
    for c in reads:
        c.start()
    for r, w in zip(reads, writes):
        r.wait()
        w.start()
    wait_all(writes)


def pack(places, base, extra):
    n = len(places)
    return pl.pallas_call(
        functools.partial(pack_kernel, n),
        out_shape=[jax.ShapeDtypeStruct((BLOCK + e, WIDE), BF16) for e in extra],
        in_specs=specs("sh"),
        out_specs=specs("h" * n),
        scratch_shapes=[pltpu.VMEM((n, BLOCK, WIDE), BF16), pltpu.SemaphoreType.DMA((2, n, 2))],
        compiler_params=params(56),
        cost_estimate=pl.CostEstimate(flops=0, bytes_accessed=2 * n * MIB, transcendentals=0),
        name="pack",
    )(jnp.stack(places), base)


def join_kernel(left, right, small, beside, partner, beside_partner, a1, a2, a3, o1, o2, o3, own, par, sem):
    copies = []
    for out, parts in ((own, (small, beside)), (par, (partner, beside_partner))):
        for h in range(2):
            copies.append(pltpu.make_async_copy(parts[h], out.at[pl.ds(h * PART, PART), :], sem))
    for o in (o1, o2, o3):
        for src, row, lane in ((left, 0, 0), (beside.at[pl.ds(TOK, 64), :], 64, 0), (right, 0, 128)):
            dst = o.at[pl.ds(BLOCK + row, src.shape[0]), pl.ds(lane, 128)]
            copies.append(pltpu.make_async_copy(src, dst, sem))
    for c in copies:
        c.start()
    wait_all(copies)


def join(left, right, small, beside, partner, beside_partner, blocks):
    pair = jax.ShapeDtypeStruct((2 * PART, 128), BF16)
    return pl.pallas_call(
        join_kernel,
        out_shape=[jax.ShapeDtypeStruct(b.shape, b.dtype) for b in blocks] + [pair, pair],
        in_specs=specs("vvvvvvhhh"),
        out_specs=specs("hhhhh"),
        scratch_shapes=[pltpu.SemaphoreType.DMA],
        input_output_aliases={6: 0, 7: 1, 8: 2},
        compiler_params=params(56),
        cost_estimate=pl.CostEstimate(flops=0, bytes_accessed=3 * MIB, transcendentals=0),
        name="join",
    )(left, right, small, beside, partner, beside_partner, *blocks)


def wait_all(copies):
    for c in copies:
        c.wait()


def specs(kinds):
    space = dict(h=pltpu.HBM, s=pltpu.SMEM, v=pltpu.VMEM)
    return [pl.BlockSpec(memory_space=space[k]) for k in kinds]


def dot(a, b):
    return jnp.dot(a, b, preferred_element_type=F32)


def unpacked(ref):
    value = ref[...]
    return jnp.concatenate([value[:, :, :64], value[:, :, 64:]], axis=1).reshape(BLOCK, 64)


def own_kernel(idx, gathered, base, acc, t_ref, own, w, left, sems):
    prompts, lefts = block_copies(idx, gathered, own, left, sems.at[4], sems.at[5])
    cols = []
    for j in range(4):
        at = pl.ds(pl.multiple_of(idx[j] * WIDE, WIDE), WIDE)
        cols.append(pltpu.make_async_copy(base.at[:, at], w.at[j], sems.at[j]))
    for c in lefts + prompts + cols:
        c.start()
    wait_all(lefts)
    factor = unpacked(left)
    wait_all(prompts)
    t_ref[...] = dot(own[...], factor)
    for j in range(4):
        cols[j].wait()
        acc[j] = dot(own[...], w[j])


def own_part(idx, gathered, base):
    return pl.pallas_call(
        own_kernel,
        out_shape=[jax.ShapeDtypeStruct((4, TOK, WIDE), F32), jax.ShapeDtypeStruct((TOK, 64), F32)],
        in_specs=specs("shh"),
        out_specs=specs("vv"),
        scratch_shapes=[
            pltpu.VMEM((TOK, BLOCK), BF16),
            pltpu.VMEM((4, BLOCK, WIDE), BF16),
            pltpu.VMEM((N_COL, 64, 128), BF16),
            pltpu.SemaphoreType.DMA((6,)),
        ],
        compiler_params=params(56),
        cost_estimate=pl.CostEstimate(flops=2 * TOK * BLOCK * 5 * WIDE, bytes_accessed=13 * MIB, transcendentals=0),
        name="own_part",
    )(idx, gathered, base)


def partner_kernel(idx, gathered, h1, h2, h3, r_ref, own_t, acc, o1, o2, o3, t_ref, par, w, part, left, sems):
    prompts, lefts = block_copies(idx, gathered, par, left, sems.at[6], sems.at[7])
    halves = [pltpu.make_async_copy(h, w.at[i], sems.at[i]) for i, h in enumerate((h1, h2, h3))]
    parts = [pltpu.make_async_copy(acc.at[i + 1], part.at[i], sems.at[3 + i]) for i in range(3)]
    for c in lefts + prompts:
        c.start()
    for h, p in zip(halves, parts):
        h.start()
        p.start()
    wait_all(lefts)
    factor = unpacked(left)
    wait_all(prompts)
    t = (own_t[...] + dot(par[...], factor)).astype(BF16)
    t_ref[...] = t
    for i, o in enumerate((o1, o2, o3)):
        right = r_ref[:, pl.ds(pl.multiple_of(idx[1 + i] % 4 * WIDE, WIDE), WIDE)]
        halves[i].wait()
        parts[i].wait()
        o[...] = (dot(par[...], w[i]) + dot(t, right) + part[i]).astype(BF16)


def partner_part(idx, gathered, halves, rights, own_t, acc):
    send = jax.ShapeDtypeStruct((TOK, WIDE), BF16)
    return pl.pallas_call(
        partner_kernel,
        out_shape=[send, send, send, jax.ShapeDtypeStruct((TOK, 64), BF16)],
        in_specs=specs("shhhhvvh"),
        out_specs=specs("vvvv"),
        scratch_shapes=[
            pltpu.VMEM((TOK, BLOCK), BF16),
            pltpu.VMEM((3, BLOCK, WIDE), BF16),
            pltpu.VMEM((3, TOK, WIDE), F32),
            pltpu.VMEM((N_COL, 64, 128), BF16),
            pltpu.SemaphoreType.DMA((8,)),
        ],
        compiler_params=params(56),
        cost_estimate=pl.CostEstimate(flops=2 * TOK * BLOCK * 4 * WIDE, bytes_accessed=12 * MIB, transcendentals=0),
        name="partner_part",
    )(idx, gathered, *halves, rights, own_t, acc)


def merge_kernel(idx, base, *refs):
    blocks, refs = refs[:7], refs[7:]
    lefts, gathered, acc, rr_ref, mag_ref, t_ref, r_ref = refs[:7]
    out, scale_ref, product, raw, comb, left, par, sems, out_sems = refs[7:]
    prompts, _ = block_copies(idx, gathered, par, None, sems.at[9], None)
    prompts.append(pltpu.make_async_copy(acc.at[0], product, sems.at[10]))
    first = []
    for j in range(8):
        for h in range(2):
            zl = idx[PLACE["zl"]] if h == 0 else 1 - idx[PLACE["zl"]]
            c = j // 2 * 4 + zl * 2 + j % 2
            for k in range(2):
                rows = pl.ds((2 * h + k) * 256, 256)
                first.append(pltpu.make_async_copy(lefts.at[j, rows, :], left.at[c, k], sems.at[8]))
    for c in first:
        c.start()
    col = pl.ds(pl.multiple_of(idx[0] * WIDE, WIDE), WIDE)
    pltpu.make_async_copy(base.at[:, col], raw.at[0], sems.at[0]).start()
    for j in range(7):
        pltpu.make_async_copy(blocks[j].at[pl.ds(0, BLOCK), :], raw.at[j + 1], sems.at[j + 1]).start()
    for c in prompts:
        c.start()
    wait_all(first)

    def part(i, squares):
        j, h = i // 2, i % 2

        @pl.when(h == 0)
        def _():
            pltpu.make_async_copy(blocks[0], raw.at[j], sems.at[j]).wait()

        factor = left[pl.ds(h * 8, 8), j % 2, pl.ds(pl.multiple_of(j // 2 * 64, 64), 64), :].reshape(512, 128)
        update = jnp.dot(factor, rr_ref[...], preferred_element_type=F32)
        for c in range(8):
            for k in range(2):
                rows = pl.ds(pl.multiple_of(h * 1024 + c * 128 + k * 64, 64), 64)
                value = raw[j, rows, :].astype(F32) + update[c * 64 : (c + 1) * 64, k * WIDE : (k + 1) * WIDE]
                comb[j, rows, :] = value
                squares += (value * value).reshape(8, 8, WIDE).sum(axis=0)
        return squares

    squares = lax.fori_loop(0, 16, part, jnp.zeros((8, WIDE), F32))
    scale = mag_ref[...] / jnp.sqrt(squares.sum(axis=0, keepdims=True) + 1e-6)
    scale_ref[...] = scale
    wait_all(prompts)
    product[...] += dot(par[...], raw[1]) + dot(t_ref[...], r_ref[...])

    def out_copy(j):
        rows = pl.ds(pl.multiple_of(idx[PLACE["rows"] + j] * BLOCK, BLOCK), BLOCK)
        return pltpu.make_async_copy(raw.at[j], out.at[rows, :], out_sems.at[j])

    @pl.loop(0, 8)
    def _(j):
        @pl.loop(0, 8)
        def _(m):
            rows = pl.ds(pl.multiple_of(m * 256, 256), 256)
            raw[j, rows, :] = (comb[j, rows, :] * scale).astype(BF16)

        out_copy(j).start()

    @pl.loop(0, 8)
    def _(j):
        out_copy(j).wait()


def merge(idx, base, blocks, lefts, gathered, acc, rr, mag, t, right):
    any_space = pl.BlockSpec(memory_space=pltpu.HBM)
    vmem = pl.BlockSpec(memory_space=pltpu.VMEM)
    return pl.pallas_call(
        merge_kernel,
        out_shape=[
            jax.ShapeDtypeStruct((8 * BLOCK, WIDE), BF16),
            jax.ShapeDtypeStruct((1, WIDE), F32),
            jax.ShapeDtypeStruct((TOK, WIDE), F32),
        ],
        in_specs=[pl.BlockSpec(memory_space=pltpu.SMEM)] + [any_space] * 11 + [vmem] * 4,
        out_specs=[any_space, vmem, vmem],
        scratch_shapes=[
            pltpu.VMEM((8, BLOCK, WIDE), BF16),
            pltpu.VMEM((8, BLOCK, WIDE), F32),
            pltpu.VMEM((N_COL, 2, 256, 128), BF16),
            pltpu.VMEM((TOK, BLOCK), BF16),
            pltpu.SemaphoreType.DMA((11,)),
            pltpu.SemaphoreType.DMA((8,)),
        ],
        compiler_params=params(56),
        cost_estimate=pl.CostEstimate(flops=2 * 128 * 512 * 8192, bytes_accessed=18 * MIB, transcendentals=0),
        name="merge",
    )(idx, base, *blocks, lefts, gathered, acc, rr, mag, t, right)


def shards(prompt, base, factor_left, factor_right, magnitude):
    row = lax.axis_index("row").astype(jnp.int32)
    zh, y = row // 4, row % 4
    order = (0,) + SHIFTS

    def served_by(dz, dy):
        return ((zh + dz) % 2) * 4 + (y + dy) % 4

    left = jnp.concatenate([factor_left[:64], factor_left[64:]], axis=1)
    small = jnp.concatenate([prompt, left], axis=0)
    right = factor_right.reshape(8, 16, 128).transpose(1, 0, 2).reshape(128, 128)

    partner, beside, beside_partner = swap(small, 64), swap(small, 2), swap(small, 66)
    relayed = {}
    places = [served_by(0, d) for d in SHIFTS] + [served_by(1, d) for d in SHIFTS + (0,)]
    slices = pack(places, base, (EXTRA, EXTRA, EXTRA + 64) + (0,) * 3 + (16,))
    packed, packed_half = dict(zip(SHIFTS, slices)), dict(zip(SHIFTS + (0,), slices[3:]))

    wave = (partner, beside, beside_partner, packed[2])
    partner, beside, beside_partner, _ = lax.optimization_barrier(wave)
    half = {d: move(after(packed_half[d], *wave), dz=1) for d in (-1, 1)}
    *blocks, prompts, prompts_partner = join(
        left, right, small, beside, partner, beside_partner, [packed[d] for d in SHIFTS]
    )
    gathered, gathered_partner = gather_x(prompts), gather_x(prompts_partner)
    straight = {d: move(block, dy=d) for d, block in zip(SHIFTS, blocks)}

    wave = (half[-1], half[1])
    for d in (1, -1):
        relayed[d] = move(after(half[d], *wave), dy=d)
    half[2] = move(after(packed_half[2], *wave), dz=1)
    got = [jnp.concatenate([left, beside[TOK:], right], axis=0)]
    for d in SHIFTS:
        below = straight[d][BLOCK : BLOCK + EXTRA]
        got.append(jnp.concatenate([below[:, :128], below[:, 128:]], axis=0))
    got = jnp.stack(got)
    places = [((zh + k) % 2) * 4 + (y - d) % 4 for d in order for k in range(2)]
    at_col = lax.axis_index("col").astype(jnp.int32)
    idx = jnp.stack([served_by(0, d) for d in order] + places + [at_col // 2 % 2])
    acc, own_t = own_part(idx, after(gathered, *wave), base)
    def rights_for(half_of_row):
        return lax.dynamic_slice_in_dim(got, 128 + half_of_row * 64, 64, 1)

    to_partner = jnp.concatenate([got[:, :128], rights_for(1 - zh)], axis=1)
    got_partner = swap(after(to_partner, *wave, own_t), 64)

    wave = (half[2], relayed[1], relayed[-1], own_t)
    half[0] = move(after(packed_half[0], *wave), dz=1)
    relayed[2] = move(after(half[2], *wave), dy=2)
    lefts = jnp.stack([got[:, :64], got_partner[:, :64], got[:, 64:128], got_partner[:, 64:128]]).reshape(1024, 128)
    lefts = gather_x(after(lefts, *wave))

    rights = jnp.stack([jnp.stack([rights_for(zh)[j], got_partner[j, 128:]]) for j in (0, 2, 3, 1)])
    rights = lax.dynamic_slice_in_dim(jnp.concatenate([rights, rights], axis=0), (4 - y) % 4, 4, 0)
    rights = lax.dynamic_slice_in_dim(jnp.concatenate([rights, rights[:, :1]], axis=1), zh, 2, 1)
    rights = rights.reshape(4, 2, 8, 8, 128).transpose(1, 0, 3, 2, 4).reshape(64, 1024)

    *sends, t = partner_part(idx, gathered_partner, [half[d] for d in SHIFTS], rights, own_t, acc)
    sums = [move(s, dy=d) for s, d in zip(sends, SHIFTS)]

    right_mine = lax.dynamic_slice(rights, (0, y * WIDE), (64, WIDE))
    rr = jnp.pad(right_mine, ((0, 64), (0, WIDE))) + jnp.pad(right_mine, ((64, 0), (WIDE, 0)))
    mag = lax.dynamic_slice(magnitude, (row * WIDE,), (WIDE,))[None]
    blocks = [half[0]]
    for d in SHIFTS:
        blocks += [straight[d], relayed[d]]
    serving, scale, product = merge(
        idx, base, blocks, lefts, gathered_partner, acc, rr, mag, t, right_mine
    )

    product = lax.optimization_barrier(product + sums[0].astype(F32)) + sums[1].astype(F32) + sums[2].astype(F32)
    return serving[None], (product * scale).astype(BF16)[None]


def solution(mesh):
    in_specs = (
        P(None, ("row", "col")),
        P("row", "col"),
        P(("row", "col"), None),
        P("row", "col"),
        P("col"),
    )
    out_specs = (P("row", None, "col"), P("row", None, "col"))
    return jax.shard_map(shards, mesh=mesh, in_specs=in_specs, out_specs=out_specs, check_vma=False)
```

```python
import functools

import jax
import jax.numpy as jnp
from jax import lax
from jax.experimental import pallas as pl
from jax.experimental.pallas import tpu as pltpu
from jax.sharding import PartitionSpec as P

AXES = ("row", "col")
SHIFTS = (1, -1, 2)
BLOCK = 2048
WIDE = 256
TOK = 1024
N_COL = 16
MIB = 1024 * 1024
F32 = jnp.float32
BF16 = jnp.bfloat16


def move(a, dz=0, dy=0):
    pairs = []
    for r in range(8):
        zh, y = divmod(r, 4)
        to = ((zh + dz) % 2) * 4 + (y + dy) % 4
        pairs += [(r * N_COL + c, to * N_COL + c) for c in range(N_COL)]
    return lax.ppermute(a, AXES, pairs)


def swap(a, bits):
    return lax.ppermute(a, AXES, [(i, i ^ bits) for i in range(128)])


def gather_x(a):
    groups = [[16 * r + 4 * x + 2 * zl + k for x in range(4) for k in range(2)] for r in range(8) for zl in range(2)]
    return lax.all_gather(a, AXES, axis=0, tiled=False, axis_index_groups=groups)


def after(x, *deps):
    return lax.optimization_barrier((x, *deps))[0]


def params(mib, **kw):
    return pltpu.CompilerParams(vmem_limit_bytes=mib * MIB, **kw)


PART = TOK + 64
PLACE = dict(served=0, rows=4, zl=12)


def block_copies(idx, gathered, whole, left, sem, left_sem):
    prompts, lefts = [], []
    for j in range(8):
        for h in range(2):
            zl = idx[PLACE["zl"]] if h == 0 else 1 - idx[PLACE["zl"]]
            c = j // 2 * 4 + zl * 2 + j % 2
            lanes = pl.ds(pl.multiple_of(c * 128, 128), 128)
            prompts.append(pltpu.make_async_copy(gathered.at[j, pl.ds(h * PART, TOK), :], whole.at[:, lanes], sem))
            if left is not None:
                lefts.append(pltpu.make_async_copy(gathered.at[j, pl.ds(h * PART + TOK, 64), :], left.at[c], left_sem))
    return prompts, lefts


EXTRA = 128


def pack_kernel(n, idx, base, *refs):
    outs, (stage, sems) = refs[:-2], refs[-2:]
    reads, writes = [], []
    for j in range(n):
        at = pl.ds(pl.multiple_of(idx[j] * WIDE, WIDE), WIDE)
        for h in range(2):
            rows = pl.ds(h * 1024, 1024)
            reads.append(pltpu.make_async_copy(base.at[rows, at], stage.at[j, rows, :], sems.at[0, j, h]))
            writes.append(pltpu.make_async_copy(stage.at[j, rows, :], outs[j].at[rows, :], sems.at[1, j, h]))
    for c in reads:
        c.start()
    for r, w in zip(reads, writes):
        r.wait()
        w.start()
    wait_all(writes)


def pack(places, base, extra):
    n = len(places)
    return pl.pallas_call(
        functools.partial(pack_kernel, n),
        out_shape=[jax.ShapeDtypeStruct((BLOCK + e, WIDE), BF16) for e in extra],
        in_specs=specs("sh"),
        out_specs=specs("h" * n),
        scratch_shapes=[pltpu.VMEM((n, BLOCK, WIDE), BF16), pltpu.SemaphoreType.DMA((2, n, 2))],
        compiler_params=params(56),
        cost_estimate=pl.CostEstimate(flops=0, bytes_accessed=2 * n * MIB, transcendentals=0),
        name="pack",
    )(jnp.stack(places), base)


def join_kernel(left, right, small, beside, partner, beside_partner, a1, a2, a3, o1, o2, o3, own, par, sem):
    copies = []
    for out, parts in ((own, (small, beside)), (par, (partner, beside_partner))):
        for h in range(2):
            copies.append(pltpu.make_async_copy(parts[h], out.at[pl.ds(h * PART, PART), :], sem))
    for o in (o1, o2, o3):
        for src, row, lane in ((left, 0, 0), (beside.at[pl.ds(TOK, 64), :], 64, 0), (right, 0, 128)):
            dst = o.at[pl.ds(BLOCK + row, src.shape[0]), pl.ds(lane, 128)]
            copies.append(pltpu.make_async_copy(src, dst, sem))
    for c in copies:
        c.start()
    wait_all(copies)


def join(left, right, small, beside, partner, beside_partner, blocks):
    pair = jax.ShapeDtypeStruct((2 * PART, 128), BF16)
    return pl.pallas_call(
        join_kernel,
        out_shape=[jax.ShapeDtypeStruct(b.shape, b.dtype) for b in blocks] + [pair, pair],
        in_specs=specs("vvvvvvhhh"),
        out_specs=specs("hhhhh"),
        scratch_shapes=[pltpu.SemaphoreType.DMA],
        input_output_aliases={6: 0, 7: 1, 8: 2},
        compiler_params=params(56),
        cost_estimate=pl.CostEstimate(flops=0, bytes_accessed=3 * MIB, transcendentals=0),
        name="join",
    )(left, right, small, beside, partner, beside_partner, *blocks)


def wait_all(copies):
    for c in copies:
        c.wait()


def specs(kinds):
    space = dict(h=pltpu.HBM, s=pltpu.SMEM, v=pltpu.VMEM)
    return [pl.BlockSpec(memory_space=space[k]) for k in kinds]


def dot(a, b):
    return jnp.dot(a, b, preferred_element_type=F32)


def unpacked(ref):
    value = ref[...]
    return jnp.concatenate([value[:, :, :64], value[:, :, 64:]], axis=1).reshape(BLOCK, 64)


def own_kernel(idx, gathered, base, acc, t_ref, own, w, left, sems):
    prompts, lefts = block_copies(idx, gathered, own, left, sems.at[4], sems.at[5])
    cols = []
    for j in range(4):
        at = pl.ds(pl.multiple_of(idx[j] * WIDE, WIDE), WIDE)
        cols.append(pltpu.make_async_copy(base.at[:, at], w.at[j], sems.at[j]))
    for c in lefts + prompts + cols:
        c.start()
    wait_all(lefts)
    factor = unpacked(left)
    wait_all(prompts)
    t_ref[...] = dot(own[...], factor)
    for j in range(4):
        cols[j].wait()
        acc[j] = dot(own[...], w[j])


def own_part(idx, gathered, base):
    return pl.pallas_call(
        own_kernel,
        out_shape=[jax.ShapeDtypeStruct((4, TOK, WIDE), F32), jax.ShapeDtypeStruct((TOK, 64), F32)],
        in_specs=specs("shh"),
        out_specs=specs("vv"),
        scratch_shapes=[
            pltpu.VMEM((TOK, BLOCK), BF16),
            pltpu.VMEM((4, BLOCK, WIDE), BF16),
            pltpu.VMEM((N_COL, 64, 128), BF16),
            pltpu.SemaphoreType.DMA((6,)),
        ],
        compiler_params=params(56),
        cost_estimate=pl.CostEstimate(flops=2 * TOK * BLOCK * 5 * WIDE, bytes_accessed=13 * MIB, transcendentals=0),
        name="own_part",
    )(idx, gathered, base)


def partner_kernel(idx, gathered, h1, h2, h3, r_ref, own_t, acc, o1, o2, o3, t_ref, par, w, part, left, sems):
    prompts, lefts = block_copies(idx, gathered, par, left, sems.at[6], sems.at[7])
    halves = [pltpu.make_async_copy(h, w.at[i], sems.at[i]) for i, h in enumerate((h1, h2, h3))]
    parts = [pltpu.make_async_copy(acc.at[i + 1], part.at[i], sems.at[3 + i]) for i in range(3)]
    for c in lefts + prompts:
        c.start()
    for h, p in zip(halves, parts):
        h.start()
        p.start()
    wait_all(lefts)
    factor = unpacked(left)
    wait_all(prompts)
    t = (own_t[...] + dot(par[...], factor)).astype(BF16)
    t_ref[...] = t
    for i, o in enumerate((o1, o2, o3)):
        right = r_ref[:, pl.ds(pl.multiple_of(idx[1 + i] % 4 * WIDE, WIDE), WIDE)]
        halves[i].wait()
        parts[i].wait()
        o[...] = (dot(par[...], w[i]) + dot(t, right) + part[i]).astype(BF16)


def partner_part(idx, gathered, halves, rights, own_t, acc):
    send = jax.ShapeDtypeStruct((TOK, WIDE), BF16)
    return pl.pallas_call(
        partner_kernel,
        out_shape=[send, send, send, jax.ShapeDtypeStruct((TOK, 64), BF16)],
        in_specs=specs("shhhhvvh"),
        out_specs=specs("vvvv"),
        scratch_shapes=[
            pltpu.VMEM((TOK, BLOCK), BF16),
            pltpu.VMEM((3, BLOCK, WIDE), BF16),
            pltpu.VMEM((3, TOK, WIDE), F32),
            pltpu.VMEM((N_COL, 64, 128), BF16),
            pltpu.SemaphoreType.DMA((8,)),
        ],
        compiler_params=params(56),
        cost_estimate=pl.CostEstimate(flops=2 * TOK * BLOCK * 4 * WIDE, bytes_accessed=12 * MIB, transcendentals=0),
        name="partner_part",
    )(idx, gathered, *halves, rights, own_t, acc)


def merge_kernel(idx, base, *refs):
    blocks, refs = refs[:7], refs[7:]
    lefts, gathered, acc, rr_ref, mag_ref, t_ref, r_ref = refs[:7]
    out, scale_ref, product, raw, comb, left, par, sems, out_sems = refs[7:]
    prompts, _ = block_copies(idx, gathered, par, None, sems.at[9], None)
    prompts.append(pltpu.make_async_copy(acc.at[0], product, sems.at[10]))
    first = []
    for j in range(8):
        for h in range(2):
            zl = idx[PLACE["zl"]] if h == 0 else 1 - idx[PLACE["zl"]]
            c = j // 2 * 4 + zl * 2 + j % 2
            for k in range(2):
                rows = pl.ds((2 * h + k) * 256, 256)
                first.append(pltpu.make_async_copy(lefts.at[j, rows, :], left.at[c, k], sems.at[8]))
    for c in first:
        c.start()
    col = pl.ds(pl.multiple_of(idx[0] * WIDE, WIDE), WIDE)
    pltpu.make_async_copy(base.at[:, col], raw.at[0], sems.at[0]).start()
    for j in range(7):
        pltpu.make_async_copy(blocks[j].at[pl.ds(0, BLOCK), :], raw.at[j + 1], sems.at[j + 1]).start()
    for c in prompts:
        c.start()
    wait_all(first)

    def part(i, squares):
        j, h = i // 2, i % 2

        @pl.when(h == 0)
        def _():
            pltpu.make_async_copy(blocks[0], raw.at[j], sems.at[j]).wait()

        factor = left[pl.ds(h * 8, 8), j % 2, pl.ds(pl.multiple_of(j // 2 * 64, 64), 64), :].reshape(512, 128)
        update = jnp.dot(factor, rr_ref[...], preferred_element_type=F32)
        for c in range(8):
            for k in range(2):
                rows = pl.ds(pl.multiple_of(h * 1024 + c * 128 + k * 64, 64), 64)
                value = raw[j, rows, :].astype(F32) + update[c * 64 : (c + 1) * 64, k * WIDE : (k + 1) * WIDE]
                comb[j, rows, :] = value
                squares += (value * value).reshape(8, 8, WIDE).sum(axis=0)
        return squares

    squares = lax.fori_loop(0, 16, part, jnp.zeros((8, WIDE), F32))
    scale = mag_ref[...] / jnp.sqrt(squares.sum(axis=0, keepdims=True) + 1e-6)
    scale_ref[...] = scale
    wait_all(prompts)
    product[...] += dot(par[...], raw[1]) + dot(t_ref[...], r_ref[...])

    def out_copy(j):
        rows = pl.ds(pl.multiple_of(idx[PLACE["rows"] + j] * BLOCK, BLOCK), BLOCK)
        return pltpu.make_async_copy(raw.at[j], out.at[rows, :], out_sems.at[j])

    @pl.loop(0, 8)
    def _(j):
        @pl.loop(0, 8)
        def _(m):
            rows = pl.ds(pl.multiple_of(m * 256, 256), 256)
            raw[j, rows, :] = (comb[j, rows, :] * scale).astype(BF16)

        out_copy(j).start()

    @pl.loop(0, 8)
    def _(j):
        out_copy(j).wait()


def merge(idx, base, blocks, lefts, gathered, acc, rr, mag, t, right):
    any_space = pl.BlockSpec(memory_space=pltpu.HBM)
    vmem = pl.BlockSpec(memory_space=pltpu.VMEM)
    return pl.pallas_call(
        merge_kernel,
        out_shape=[
            jax.ShapeDtypeStruct((8 * BLOCK, WIDE), BF16),
            jax.ShapeDtypeStruct((1, WIDE), F32),
            jax.ShapeDtypeStruct((TOK, WIDE), F32),
        ],
        in_specs=[pl.BlockSpec(memory_space=pltpu.SMEM)] + [any_space] * 11 + [vmem] * 4,
        out_specs=[any_space, vmem, vmem],
        scratch_shapes=[
            pltpu.VMEM((8, BLOCK, WIDE), BF16),
            pltpu.VMEM((8, BLOCK, WIDE), F32),
            pltpu.VMEM((N_COL, 2, 256, 128), BF16),
            pltpu.VMEM((TOK, BLOCK), BF16),
            pltpu.SemaphoreType.DMA((11,)),
            pltpu.SemaphoreType.DMA((8,)),
        ],
        compiler_params=params(56),
        cost_estimate=pl.CostEstimate(flops=2 * 128 * 512 * 8192, bytes_accessed=18 * MIB, transcendentals=0),
        name="merge",
    )(idx, base, *blocks, lefts, gathered, acc, rr, mag, t, right)


def shards(prompt, base, factor_left, factor_right, magnitude):
    row = lax.axis_index("row").astype(jnp.int32)
    zh, y = row // 4, row % 4
    order = (0,) + SHIFTS

    def served_by(dz, dy):
        return ((zh + dz) % 2) * 4 + (y + dy) % 4

    left = jnp.concatenate([factor_left[:64], factor_left[64:]], axis=1)
    small = jnp.concatenate([prompt, left], axis=0)
    right = factor_right.reshape(8, 16, 128).transpose(1, 0, 2).reshape(128, 128)

    partner, beside, beside_partner = swap(small, 64), swap(small, 2), swap(small, 66)
    relayed = {}
    places = [served_by(0, d) for d in SHIFTS] + [served_by(1, d) for d in SHIFTS + (0,)]
    slices = pack(places, base, (EXTRA, EXTRA, EXTRA + 16) + (0,) * 3 + (16,))
    packed, packed_half = dict(zip(SHIFTS, slices)), dict(zip(SHIFTS + (0,), slices[3:]))

    wave = (partner, beside, beside_partner, packed[2])
    partner, beside, beside_partner, _ = lax.optimization_barrier(wave)
    half = {d: move(after(packed_half[d], *wave), dz=1) for d in (-1, 1)}
    *blocks, prompts, prompts_partner = join(
        left, right, small, beside, partner, beside_partner, [packed[d] for d in SHIFTS]
    )
    gathered, gathered_partner = gather_x(prompts), gather_x(prompts_partner)
    straight = {d: move(block, dy=d) for d, block in zip(SHIFTS, blocks)}

    wave = (half[-1], half[1])
    for d in (1, -1):
        relayed[d] = move(after(half[d], *wave), dy=d)
    half[2] = move(after(packed_half[2], *wave), dz=1)
    got = [jnp.concatenate([left, beside[TOK:], right], axis=0)]
    for d in SHIFTS:
        below = straight[d][BLOCK : BLOCK + EXTRA]
        got.append(jnp.concatenate([below[:, :128], below[:, 128:]], axis=0))
    got = jnp.stack(got)
    places = [((zh + k) % 2) * 4 + (y - d) % 4 for d in order for k in range(2)]
    at_col = lax.axis_index("col").astype(jnp.int32)
    idx = jnp.stack([served_by(0, d) for d in order] + places + [at_col // 2 % 2])
    acc, own_t = own_part(idx, after(gathered, *wave), base)
    def rights_for(half_of_row):
        return lax.dynamic_slice_in_dim(got, 128 + half_of_row * 64, 64, 1)

    to_partner = jnp.concatenate([got[:, :128], rights_for(1 - zh)], axis=1)
    got_partner = swap(after(to_partner, *wave, own_t), 64)

    wave = (half[2], relayed[1], relayed[-1], own_t)
    half[0] = move(after(packed_half[0], *wave), dz=1)
    relayed[2] = move(after(half[2], *wave), dy=2)
    lefts = jnp.stack([got[:, :64], got_partner[:, :64], got[:, 64:128], got_partner[:, 64:128]]).reshape(1024, 128)
    lefts = gather_x(after(lefts, *wave))

    rights = jnp.stack([jnp.stack([rights_for(zh)[j], got_partner[j, 128:]]) for j in (0, 2, 3, 1)])
    rights = lax.dynamic_slice_in_dim(jnp.concatenate([rights, rights], axis=0), (4 - y) % 4, 4, 0)
    rights = lax.dynamic_slice_in_dim(jnp.concatenate([rights, rights[:, :1]], axis=1), zh, 2, 1)
    rights = rights.reshape(4, 2, 8, 8, 128).transpose(1, 0, 3, 2, 4).reshape(64, 1024)

    *sends, t = partner_part(idx, gathered_partner, [half[d] for d in SHIFTS], rights, own_t, acc)
    sums = [move(s, dy=d) for s, d in zip(sends, SHIFTS)]

    right_mine = lax.dynamic_slice(rights, (0, y * WIDE), (64, WIDE))
    rr = jnp.pad(right_mine, ((0, 64), (0, WIDE))) + jnp.pad(right_mine, ((64, 0), (WIDE, 0)))
    mag = lax.dynamic_slice(magnitude, (row * WIDE,), (WIDE,))[None]
    blocks = [half[0]]
    for d in SHIFTS:
        blocks += [straight[d], relayed[d]]
    serving, scale, product = merge(
        idx, base, blocks, lefts, gathered_partner, acc, rr, mag, t, right_mine
    )

    product = lax.optimization_barrier(product + sums[0].astype(F32)) + sums[1].astype(F32) + sums[2].astype(F32)
    return serving[None], (product * scale).astype(BF16)[None]


def solution(mesh):
    in_specs = (
        P(None, ("row", "col")),
        P("row", "col"),
        P(("row", "col"), None),
        P("row", "col"),
        P("col"),
    )
    out_specs = (P("row", None, "col"), P("row", None, "col"))
    return jax.shard_map(shards, mesh=mesh, in_specs=in_specs, out_specs=out_specs, check_vma=False)
```
